32 devices in a mesh: groups: 2 (over x), rows: 16 (over z, y, core).
Axes of the slice: x: 2, y: 2, z: 4, core: 2. Of those that a mesh axis runs over, the one named last changes fastest.
Arguments:
- queries: bfloat16 [1024, 4096], P(('groups', 'rows')), parts along dimension 0, may hold values from -200 to 200
- cache_keys: bfloat16 [1024, 2, 128, 128], P(('groups', 'rows')), parts along dimension 0, may hold values from -6 to 6
- cache_values: bfloat16 [1024, 2, 128, 128], P(('groups', 'rows')), parts along dimension 0, may hold values from -6 to 6
- lengths: int32 [1024], P(('groups', 'rows')), parts along dimension 0, may hold values from 2 to 128, as said below
- hidden: bfloat16 [1024, 2048], P(('groups', 'rows')), parts along dimension 0, may hold values from -6 to 6
- out_weight: bfloat16 [4096, 2048], P('rows'), may hold values from -0.1875 to 0.1875
- norm_gain: float32 [2048], replicated, may hold values from 0.25 to 1.75
- w_gate: bfloat16 [16, 2048, 768], P('rows'), may hold values from -0.125 to 0.125
- w_up: bfloat16 [16, 2048, 768], P('rows'), may hold values from -0.125 to 0.125
- w_down: bfloat16 [16, 768, 2048], P('rows'), may hold values from -0.3125 to 0.3125
- expert_ids: int32 [1024, 8], P(('groups', 'rows')), parts along dimension 0, may hold values from 0 to 15, all different within a row; in each aligned block of 32 rows (0 to 31, 32 to 63, ...) at most 32 rows name the same one
- gate_numer: int32 [1024, 8], P(('groups', 'rows')), parts along dimension 0, may hold values from 1 to 384, 1024 in all within a row
Outputs:
- layer_out: bfloat16 [1024, 2048], P(('groups', 'rows')), parts along dimension 0
The draws below stay inside these ranges and needn't reach their ends.
There are 2 independent parts, one for each index of `groups`. The reference program is written for one: setup_inputs(seed, part) draws one part's arguments, and reference() takes and returns one part's arrays. A program takes and returns all parts, laid end to end along the dimension named above; an argument that names none is the same for every part. Nothing has to cross between parts.
Inputs may be any that keep to these rules, and one draw needn't show every extreme that they name: `expert_ids`: in the rows of one device no expert is named more than 32 times; in some device's rows some expert is named exactly 32 times. The 8 experts of a row differ. `gate_numer`: the 8 numerators of a row sum to 1024; the largest is 384. `lengths`: some row has all 128 slots live.
All inputs are finite; a program needn't handle non-finite values.
Results may differ from the reference program's by a relative error of at most 0.006.
Values may be sent and summed in bfloat16 or wider, within the bound.
No kernel may reach another device: no remote copies, remote signals or barrier semaphores. Data moves between devices by JAX's collectives and lax.ppermute only.
A program may use at most 128 MiB of HBM per device.

```python
import math
import jax
import jax.numpy as jnp
import numpy as np
from jax import lax

D = 2048
FF = 768
KV_HEADS = 2
HEAD = 128
TOPK = 8
TOK_DEV = 32
CACHE = 128
EXPERTS = 16
TOKENS = 512
FEAT = 4096
CAP = 32
N_ROWS = 16


def shared_normals(key):
    key_common = jax.random.fold_in(key, 101)
    base = jax.random.normal(key_common, (TOKENS, KV_HEADS, CACHE, HEAD), jnp.float32)
    return jnp.clip(base, -6.0, 6.0)


def draw_cache_keys(key, part):
    base = shared_normals(key)
    return base.astype(jnp.bfloat16)


def draw_queries(key, part):
    key = jax.random.fold_in(key, 7)
    noise_part = jnp.clip(jax.random.normal(key, (TOKENS, FEAT), jnp.float32), -6.0, 6.0)
    return noise_part.astype(jnp.bfloat16)


def draw_lengths(key, part):
    key = jax.random.fold_in(key, 13)
    drawn = jax.random.randint(key, (TOKENS,), 2, CACHE + 1, dtype=jnp.int32)
    row_index = jnp.arange(TOKENS, dtype=jnp.int32)
    return jnp.where(row_index % 7 == 3, CACHE, drawn).astype(jnp.int32)


def block_levels(stream_key, extent, shards, low, top_value):
    def one(dim, parts):
        steps = jax.random.uniform(jax.random.fold_in(jax.random.fold_in(stream_key, 6), dim), (parts,), jnp.float32, low / len(shards), top_value / len(shards))
        return jnp.repeat(jnp.exp(steps), extent[dim] // parts).reshape((-1,) + (1,) * (len(extent) - dim - 1))

    loudness = one(*shards[0])
    for cut in shards[1:]:
        loudness = loudness * one(*cut)
    return loudness


def profile(count, total, most, slope):
    portions = [(1 << 20) // math.isqrt(grade ** slope) + 1 for grade in range(2, count + 1)]
    rest, counts = total - most - (count - 1), [1] * (count - 1)
    while rest > 0:
        free = [i for i in range(count - 1) if counts[i] < most]
        mass, budget = sum([portions[i] for i in free]), rest
        for i in free:
            more = min(most - counts[i], max(1, budget * portions[i] // mass), rest)
            counts[i] = counts[i] + more
            rest = rest - more
    return np.array([most] + counts)


def uneven_parts(stream_key, count, total, limit, slope):
    if count == 2:
        one = jax.random.randint(stream_key, (), max(1, total - limit), min(limit, total - 1) + 1)
        return jnp.stack([one, total - one])
    tallies = jnp.asarray(profile(count, total, limit, slope), jnp.int32)
    pairs = (count - 1) // 2
    donor, sink = tallies[1:1 + 2 * pairs:2], tallies[2:2 + 2 * pairs:2]
    slack = jnp.minimum(donor - 1, limit - sink)
    shifted = jax.random.randint(jax.random.fold_in(stream_key, 1), (pairs,), 0, 1 << 20) % (slack + 1)
    tallies = tallies.at[1:1 + 2 * pairs:2].set(donor - shifted).at[2:2 + 2 * pairs:2].set(sink + shifted)
    return tallies[jax.random.permutation(jax.random.fold_in(stream_key, 2), count)]


def shared_out(key, own, number, rows, amount, top, most, lean):
    ranking = jax.random.permutation(key, amount)
    heavy_load, ordinary = portions_of(amount, rows * top, most, lean, True), portions_of(amount, rows * top, most, lean, False)
    places = jnp.arange(amount)

    def named(tallies, turn):
        used = int((tallies > 0).sum())
        fixed = max(1, used // 4)
        passed = fixed + (places - fixed + turn * (used - fixed)) % max(1, amount - fixed)
        return jnp.zeros((amount,), jnp.int32).at[ranking[jnp.where(places < fixed, places, passed)]].set(jnp.asarray(tallies, jnp.int32))

    tallies = jnp.where(number % 4 == 0, named(heavy_load, number // 4), named(ordinary, number - number // 4 - 1))
    mixed = jax.random.permutation(jax.random.fold_in(own, 3), amount)
    source_of, sink = mixed[0:amount // 2 * 2:2], mixed[1:amount // 2 * 2:2]
    margin = jnp.minimum(tallies[source_of] - 1, most - tallies[sink]) // 2
    margin = jnp.where((source_of == ranking[0]) | (sink == ranking[0]) | (tallies[sink] == 0), 0, jnp.maximum(margin, 0))
    passed = jax.random.randint(jax.random.fold_in(own, 4), (amount // 2,), 0, 1 << 20) % (margin + 1)
    tallies = tallies.at[source_of].add(-passed).at[sink].add(passed)
    labels = jnp.searchsorted(jnp.cumsum(tallies), jnp.arange(rows * top), side="right").astype(jnp.int32)
    table = labels.reshape(top, rows).T
    table = table[jax.random.permutation(jax.random.fold_in(own, 1), rows)]
    turn = jax.random.randint(jax.random.fold_in(own, 2), (rows, 1), 0, top)
    return jnp.take_along_axis(table, (jnp.arange(top)[None, :] + turn) % top, axis=1)


def portions_of(count, total, limit, skew, full):
    loads = [(1 << 20) // math.isqrt(standing ** skew) + 1 for standing in range(1, count + 1)]
    largest = limit if full else min(limit, max(-(-total // count), total * loads[0] // sum(loads)))
    least = 1 if total - largest >= count - 1 else 0
    counts, rest = [largest] + [least] * (count - 1), total - largest - least * (count - 1)
    while rest > 0:
        movable = [i for i in range(1, count) if counts[i] < largest] or [i for i in range(1, count) if counts[i] < limit]
        whole, left = sum([loads[i] for i in movable]), rest
        for i in movable:
            more = min(limit - counts[i], max(1, left * loads[i] // whole), rest)
            counts[i] = counts[i] + more
            rest = rest - more
    return np.array(counts)


def noise(rng, extent, spread, most, split=(), kind=jnp.bfloat16):
    level = block_levels(rng, extent, split, -0.22, 0.18) if split else 1.0
    entries = jax.random.normal(rng, extent, jnp.float32) * spread * level
    return jnp.minimum(jnp.maximum(entries, -most), most).astype(kind)


def setup_inputs(seed: int = 0, part: int = 0) -> dict:
    streams_of = jax.random.split(jax.random.key(seed), 13)
    own_keys = jax.random.split(jax.random.fold_in(streams_of[12], part), 13)
    queries = draw_queries(jax.random.fold_in(jax.random.fold_in(streams_of[12], part), 71), part)
    cache_keys = draw_cache_keys(jax.random.fold_in(jax.random.fold_in(streams_of[12], part), 71), part)
    cache_values = noise(own_keys[2], (TOKENS, KV_HEADS, CACHE, HEAD), 1.0, 6.0, ((0, 16),))
    lengths = draw_lengths(jax.random.fold_in(jax.random.fold_in(streams_of[12], part), 71), part)
    hidden = noise(own_keys[4], (TOKENS, D), 1.0, 6.0, ((0, 16),))
    out_weight = noise(streams_of[5], (FEAT, D), (FEAT // 4) ** -0.5, 0.1875, ((0, 16),))
    norm_gain = jnp.clip(1.0 + 0.15 * jax.random.normal(streams_of[6], (D,), jnp.float32), 0.25, 1.75)
    w_gate = noise(streams_of[7], (EXPERTS, D, FF), D ** -0.5, 0.125, ((0, 16),))
    w_up = noise(streams_of[8], (EXPERTS, D, FF), D ** -0.5, 0.125, ((0, 16),))
    w_down = noise(streams_of[9], (EXPERTS, FF, D), (FF // 2) ** -0.5, 0.3125, ((0, 16),))
    expert_ids_keys = jax.random.split(jax.random.fold_in(own_keys[10], 1), TOKENS // TOK_DEV)
    expert_ids_turns = jax.random.permutation(jax.random.fold_in(own_keys[10], 3), TOKENS // TOK_DEV)
    expert_ids = jax.vmap(lambda own, number: shared_out(jax.random.fold_in(own_keys[10], 2), own, number, TOK_DEV, EXPERTS, TOPK, CAP, 2))(expert_ids_keys, expert_ids_turns).reshape((TOKENS, TOPK))
    gate_numer = jax.vmap(lambda own: uneven_parts(own, TOPK, 1024, 384, 0))(jax.random.split(own_keys[11], TOKENS)).reshape((TOKENS, TOPK)).astype(jnp.int32)
    return {"queries": queries, "cache_keys": cache_keys, "cache_values": cache_values, "lengths": lengths, "hidden": hidden, "out_weight": out_weight, "norm_gain": norm_gain, "w_gate": w_gate, "w_up": w_up, "w_down": w_down, "expert_ids": expert_ids, "gate_numer": gate_numer}


gate_scale = 1.0 / 1024.0

def attend(queries, cache_keys, cache_values, lengths):
    row_count, kv_count, cache_len, head_size = cache_keys.shape
    grouped = queries.astype(jnp.float32).reshape(row_count, kv_count, -1, head_size)
    scores = jnp.einsum('rkgh,rkch->rkgc', grouped, cache_keys.astype(jnp.float32)) * (1.0 / math.sqrt(head_size))
    visible = jnp.arange(cache_len, dtype=jnp.int32)[None, None, None, :] < lengths[:, None, None, None]
    scores = jnp.where(visible, scores, -1e+30)
    highest = lax.optimization_barrier(jnp.max(scores, axis=3, keepdims=True))
    weights = jnp.exp(scores - highest)
    shares = (weights / lax.optimization_barrier(jnp.sum(weights, axis=3, keepdims=True))).astype(jnp.bfloat16)
    blended = jnp.einsum('rkgc,rkch->rkgh', shares.astype(jnp.float32), cache_values.astype(jnp.float32))
    return blended.reshape(row_count, -1).astype(jnp.bfloat16)

def rms_scale(features, norm_gain):
    mean_square = lax.optimization_barrier(jnp.mean(features * features, axis=-1, keepdims=True))
    return features * lax.rsqrt(mean_square + 1e-06) * norm_gain

def serve_expert(operands):
    rows_in, gate_w, up_w, down_w = operands
    gate_proj = jnp.dot(rows_in, gate_w, preferred_element_type=jnp.float32)
    raised = jnp.dot(rows_in, up_w, preferred_element_type=jnp.float32)
    inner_act = (jax.nn.silu(gate_proj) * raised).astype(jnp.bfloat16)
    return jnp.dot(inner_act, down_w, preferred_element_type=jnp.float32).astype(jnp.bfloat16)

def reference(queries, cache_keys, cache_values, lengths, hidden, out_weight, norm_gain, w_gate, w_up, w_down, expert_ids, gate_numer):
    attended = attend(queries, cache_keys, cache_values, lengths)
    projected = jnp.dot(attended, out_weight, preferred_element_type=jnp.float32)
    residual = (hidden.astype(jnp.float32) + projected).astype(jnp.bfloat16)
    normed = rms_scale(residual.astype(jnp.float32), norm_gain).astype(jnp.bfloat16)
    pairs_dev = TOK_DEV * TOPK
    grouped_ids = expert_ids.reshape(N_ROWS, pairs_dev)
    one_hot = (grouped_ids[:, :, None] == jnp.arange(EXPERTS, dtype=jnp.int32)[None, None, :]).astype(jnp.int32)
    position = lax.optimization_barrier(jnp.sum(jnp.cumsum(one_hot, axis=1) * one_hot, axis=2)) - 1
    target = (grouped_ids * CAP + position).astype(jnp.int32)
    pair_rows = jnp.broadcast_to(normed.reshape(N_ROWS, TOK_DEV, 1, D), (N_ROWS, TOK_DEV, TOPK, D)).reshape(N_ROWS, pairs_dev, D)
    source = jnp.broadcast_to(jnp.arange(N_ROWS, dtype=jnp.int32)[:, None], (N_ROWS, pairs_dev))
    buffers = jnp.zeros((N_ROWS, EXPERTS * CAP, D), jnp.bfloat16).at[source, target].set(pair_rows)
    by_expert = buffers.reshape(N_ROWS, EXPERTS, CAP, D).transpose(1, 0, 2, 3).reshape(EXPERTS, N_ROWS * CAP, D)
    served = lax.map(serve_expert, (by_expert, w_gate, w_up, w_down))
    returned = served.reshape(EXPERTS, N_ROWS, CAP, D).transpose(1, 0, 2, 3).reshape(N_ROWS, EXPERTS * CAP, D)
    picked = returned[source, target].reshape(TOKENS, TOPK, D)
    gate_values = gate_numer.astype(jnp.float32) * gate_scale
    combined = jnp.zeros((TOKENS, D), jnp.float32)
    for slot_index in range(TOPK):
        combined = combined + gate_values[:, slot_index, None] * picked[:, slot_index].astype(jnp.float32)
    return (residual.astype(jnp.float32) + combined).astype(jnp.bfloat16)
```

```python
import math

import jax
import jax.numpy as jnp
from jax import lax
from jax.sharding import PartitionSpec as P

TOPK = 8
BF16 = jnp.bfloat16
F32 = jnp.float32


gate_scale = 1.0 / 1024.0


def attend(queries, cache_keys, cache_values, lengths):
    row_count, kv_count, cache_len, head_size = cache_keys.shape
    grouped = queries.reshape(row_count, kv_count, -1, head_size)
    scores = jnp.einsum(
        "rkgh,rkch->rkgc", grouped, cache_keys, preferred_element_type=jnp.float32
    ) * (1.0 / math.sqrt(head_size))
    visible = (
        lax.broadcasted_iota(jnp.int32, (1, 1, 1, cache_len), 3) < lengths[:, None, None, None]
    )
    scores = jnp.where(visible, scores, -1e30)
    highest = jnp.max(scores, axis=3, keepdims=True)
    weights = jnp.exp(scores - highest)
    shares = (weights / jnp.sum(weights, axis=3, keepdims=True)).astype(jnp.bfloat16)
    blended = jnp.einsum(
        "rkgc,rkch->rkgh", shares, cache_values, preferred_element_type=jnp.float32
    )
    return blended.reshape(row_count, -1).astype(jnp.bfloat16)


def rms_scale(features, norm_gain):
    mean_square = jnp.mean(features * features, axis=-1, keepdims=True)
    return features * lax.rsqrt(mean_square + 1e-06) * norm_gain


def ring_plan(devices):
    chips = devices // 2
    order = list(range(0, chips, 2)) + list(range(chips - 1, 0, -2))
    ahead, swap = [], []
    for place in range(chips):
        here, after = order[place], order[(place + 1) % chips]
        ahead += [(2 * here, 2 * after), (2 * after + 1, 2 * here + 1)]
        swap += [(2 * here, 2 * here + 1), (2 * here + 1, 2 * here)]
    back = [(target, source) for source, target in ahead]
    return order, ahead, back, swap


def ring_sum(parts, perm):
    message = parts[0].astype(BF16)
    half = message.shape[0]
    for part in parts[1:]:
        message = lax.ppermute(message, "rows", perm).astype(F32)
        if message.shape[0] == half:
            message = jnp.concatenate([message + part[:half], part[half:]], axis=0)
        else:
            message = message + part
        message = message.astype(BF16)
    return lax.ppermute(message, "rows", perm).astype(F32)


def on_device(
    queries,
    cache_keys,
    cache_values,
    lengths,
    hidden,
    out_weight,
    norm_gain,
    w_gate,
    w_up,
    w_down,
    expert_ids,
    gate_numer,
):
    rows, width = hidden.shape
    devices = lax.axis_size("rows")
    chips, hops = devices // 2, devices // 4
    local_experts = w_gate.shape[0]
    expert_total = local_experts * devices
    order, ahead, back, swap = ring_plan(devices)
    spot = [0] * chips
    for place, chip in enumerate(order):
        spot[chip] = place
    me = lax.axis_index("rows")
    chip, core = me // 2, me % 2
    place = jnp.asarray(spot, jnp.int32)[chip]
    sign = 1 - 2 * core

    def chip_at(offset):
        return jnp.asarray(order, jnp.int32)[(place + sign * offset) % chips]

    def paired(array):
        other = lax.ppermute(array, "rows", swap)
        return other

    weight_other = paired(out_weight)
    experts_own = (w_gate, w_up, w_down)
    experts_other = tuple(paired(w) for w in experts_own)
    hidden_other = paired(hidden)

    choice = lax.broadcasted_iota(jnp.int32, (1, 1, expert_total), 2)
    gates = jnp.sum(
        jnp.where(expert_ids[:, :, None] == choice, gate_numer[:, :, None], 0), axis=1
    ).astype(F32) * gate_scale
    all_gates = lax.all_gather(gates, "rows", axis=0, tiled=True)
    all_gates = all_gates.reshape(chips, 2, rows, expert_total)

    attended = attend(queries, cache_keys, cache_values, lengths)
    chip_feats = attended.shape[1] // chips
    feats = chip_feats // 2
    tokens = attended.reshape(rows, chips, chip_feats).transpose(1, 0, 2)
    groups = [[2 * c + k for c in range(chips)] for k in range(2)]
    tokens = lax.all_to_all(
        tokens, "rows", split_axis=0, concat_axis=0, tiled=True, axis_index_groups=groups
    )
    mine = jnp.take(tokens, jnp.stack([chip_at(o) for o in range(hops, -1, -1)]), axis=0)
    give = jnp.take(tokens, jnp.stack([chip_at(-o) for o in range(hops - 1, 0, -1)]), axis=0)
    got = paired(give)
    pieces = [mine[0]]
    for step in range(1, hops):
        pieces += [mine[step], got[step - 1]]
    pieces.append(mine[hops])
    lhs = jnp.concatenate(pieces, axis=0)
    weight = jnp.where(
        core == 0,
        jnp.concatenate([out_weight, weight_other], axis=0),
        jnp.concatenate([weight_other, out_weight], axis=0),
    )
    partial = jnp.dot(lhs, weight, preferred_element_type=F32)

    def blocks_of(array):
        out = [array[:rows]]
        for step in range(1, hops):
            start = rows + (step - 1) * 2 * rows
            out.append(array[start : start + 2 * rows])
        return out, array[rows + (hops - 1) * 2 * rows :]

    far, own = blocks_of(partial)
    total = ring_sum(far, ahead)
    total = jnp.concatenate([total[:rows] + own, total[rows:]], axis=0)
    got = paired(total)
    projected = total + jnp.concatenate([got[rows:], got[:rows]], axis=0)
    hidden_pair = jnp.concatenate([hidden, hidden_other], axis=0)
    residual = (hidden_pair.astype(F32) + projected).astype(BF16)
    normed = rms_scale(residual.astype(F32), norm_gain).astype(BF16)

    held = normed
    arrived = [normed[:rows]]
    for step in range(1, hops + 1):
        if step == hops:
            held = held[:rows]
        held = lax.ppermute(held, "rows", ahead)
        arrived.append(held)
    lhs = jnp.concatenate(arrived[::-1], axis=0)

    def gate_block(offset, parity):
        return all_gates[chip_at(-offset), parity]

    gate_rows = [gate_block(hops, core)]
    for step in range(hops - 1, 0, -1):
        gate_rows += [gate_block(step, core), gate_block(step, 1 - core)]
    gate_rows.append(gate_block(0, core))
    gate_rows = jnp.concatenate(gate_rows, axis=0)
    expert_iota = lax.broadcasted_iota(jnp.int32, (1, expert_total), 1)

    served = 0.0
    for owner, group in ((me, experts_own), (chip * 2 + 1 - core, experts_other)):
        for k in range(local_experts):
            w_g, w_u, w_d = (w[k] for w in group)
            gate_proj = jnp.dot(lhs, w_g, preferred_element_type=F32)
            raised = jnp.dot(lhs, w_u, preferred_element_type=F32)
            inner = (jax.nn.silu(gate_proj) * raised).astype(BF16)
            done = jnp.dot(inner, w_d, preferred_element_type=F32).astype(BF16)
            share = jnp.sum(
                jnp.where(expert_iota == owner * local_experts + k, gate_rows, 0.0),
                axis=1,
                keepdims=True,
            )
            served = served + share * done.astype(F32)

    far, own = blocks_of(served)
    total = ring_sum(far, back)
    got = paired(total[rows:])
    combined = total[:rows] + own + got
    return (residual[:rows].astype(F32) + combined).astype(BF16)


def solution(mesh):
    in_specs = (
        P(("groups", "rows"), None),
        P(("groups", "rows"), None, None, None),
        P(("groups", "rows"), None, None, None),
        P(("groups", "rows")),
        P(("groups", "rows"), None),
        P("rows", None),
        P(),
        P("rows", None, None),
        P("rows", None, None),
        P("rows", None, None),
        P(("groups", "rows"), None),
        P(("groups", "rows"), None),
    )
    out_specs = P(("groups", "rows"), None)
    return jax.shard_map(
        on_device, mesh=mesh, in_specs=in_specs, out_specs=out_specs, check_vma=False
    )
```

```python
import functools
import math

import jax
import jax.numpy as jnp
from jax import lax
from jax.experimental import pallas as pl
from jax.experimental.pallas import tpu as pltpu
from jax.sharding import PartitionSpec as P

TOPK = 8
BF16 = jnp.bfloat16
F32 = jnp.float32


gate_scale = 1.0 / 1024.0


def attend(queries, cache_keys, cache_values, lengths):
    row_count, kv_count, cache_len, head_size = cache_keys.shape
    grouped = queries.reshape(row_count, kv_count, -1, head_size)
    scores = jnp.einsum(
        "rkgh,rkch->rkgc", grouped, cache_keys, preferred_element_type=jnp.float32
    ) * (1.0 / math.sqrt(head_size))
    visible = (
        lax.broadcasted_iota(jnp.int32, (1, 1, 1, cache_len), 3) < lengths[:, None, None, None]
    )
    scores = jnp.where(visible, scores, -1e30)
    highest = jnp.max(scores, axis=3, keepdims=True)
    weights = jnp.exp(scores - highest)
    shares = (weights / jnp.sum(weights, axis=3, keepdims=True)).astype(jnp.bfloat16)
    blended = jnp.einsum(
        "rkgc,rkch->rkgh", shares, cache_values, preferred_element_type=jnp.float32
    )
    return blended.reshape(row_count, -1).astype(jnp.bfloat16)


def rms_scale(features, norm_gain):
    mean_square = jnp.mean(features * features, axis=-1, keepdims=True)
    return features * lax.rsqrt(mean_square + 1e-06) * norm_gain


def ring_plan(devices):
    chips = devices // 2
    order = list(range(0, chips, 2)) + list(range(chips - 1, 0, -2))
    swap = [(device, device ^ 1) for device in range(devices)]

    def toward(step):
        pairs = []
        for place in range(chips):
            for core in range(2):
                target = order[(place + step * (1 - 2 * core)) % chips]
                pairs.append((2 * order[place] + core, 2 * target + core))
        return pairs

    return order, toward, swap


def project_kernel(core_ref, x_ref, own_ref, other_ref, out_ref):
    feats = own_ref.shape[0]

    def both(first, second):
        out_ref[...] = jnp.dot(
            x_ref[:, :feats], first[...], preferred_element_type=F32
        ) + jnp.dot(x_ref[:, feats : 2 * feats], second[...], preferred_element_type=F32)

    @pl.when(core_ref[0] == 0)
    def _():
        both(own_ref, other_ref)

    @pl.when(core_ref[0] == 1)
    def _():
        both(other_ref, own_ref)


def project(core, tokens, own, other):
    rows, feats, width = tokens.shape[0], own.shape[0], own.shape[1]
    vmem = pl.BlockSpec(memory_space=pltpu.VMEM)
    return pl.pallas_call(
        project_kernel,
        out_shape=jax.ShapeDtypeStruct((rows, width), F32),
        in_specs=[pl.BlockSpec(memory_space=pltpu.SMEM), vmem, vmem, vmem],
        out_specs=vmem,
        compiler_params=pltpu.CompilerParams(vmem_limit_bytes=24 * 1024 * 1024),
        cost_estimate=pl.CostEstimate(
            flops=4 * rows * feats * width, bytes_accessed=4 * feats * width, transcendentals=0
        ),
    )(core, tokens, own, other)


def expert_kernel(tiles, pieces, *refs):
    piece_refs, refs = refs[:pieces], refs[pieces:]
    gates_ref, own_refs, other_refs = refs[0], refs[1:4], refs[4:7]
    out_ref, far_ref, x_ref = refs[7:]
    step = pl.program_id(0)

    @pl.when(step == 0)
    def _():
        start = 0
        for piece in piece_refs:
            x_ref[start : start + piece.shape[0], :] = piece[...]
            start += piece.shape[0]
        out_ref[...] = jnp.zeros_like(out_ref)

    def serve(weight_refs, column):
        w_gate, w_up, w_down = weight_refs
        gate_proj = jnp.dot(x_ref[...], w_gate[0], preferred_element_type=F32)
        raised = jnp.dot(x_ref[...], w_up[0], preferred_element_type=F32)
        inner = (jax.nn.silu(gate_proj) * raised).astype(BF16)
        done = jnp.dot(inner, w_down[0], preferred_element_type=F32)
        out_ref[...] += gates_ref[:, column : column + 1] * done

    @pl.when(step < tiles)
    def _():
        serve(own_refs, 0)

    @pl.when(step >= tiles)
    def _():
        serve(other_refs, 1)

    @pl.when(step == 2 * tiles - 1)
    def _():
        far_ref[...] = out_ref[: far_ref.shape[0], :].astype(BF16)


def experts(pieces, gates, own, other, local):
    width, hidden_units = own[0].shape[1:]
    rows = sum(piece.shape[0] for piece in pieces)
    far = pieces[0].shape[0]
    tile = 256
    tiles = hidden_units // tile

    def specs(place):
        wide = pl.BlockSpec((1, width, tile), lambda t: (local, 0, place(t)))
        tall = pl.BlockSpec((1, tile, width), lambda t: (local, place(t), 0))
        return [wide, wide, tall]

    whole = pl.BlockSpec(memory_space=pltpu.VMEM)
    return pl.pallas_call(
        functools.partial(expert_kernel, tiles, len(pieces)),
        out_shape=(
            jax.ShapeDtypeStruct((rows, width), F32),
            jax.ShapeDtypeStruct((far, width), BF16),
        ),
        grid=(2 * tiles,),
        in_specs=[whole] * (len(pieces) + 1)
        + specs(lambda t: jnp.minimum(t, tiles - 1))
        + specs(lambda t: jnp.maximum(t - tiles, 0)),
        out_specs=(whole, whole),
        scratch_shapes=[pltpu.VMEM((rows, width), BF16)],
        compiler_params=pltpu.CompilerParams(vmem_limit_bytes=48 * 1024 * 1024),
        cost_estimate=pl.CostEstimate(
            flops=12 * rows * hidden_units * width,
            bytes_accessed=12 * hidden_units * width,
            transcendentals=2 * rows * hidden_units,
        ),
    )(*pieces, gates, *own, *other)


def on_device(
    queries,
    cache_keys,
    cache_values,
    lengths,
    hidden,
    out_weight,
    norm_gain,
    w_gate,
    w_up,
    w_down,
    expert_ids,
    gate_numer,
):
    rows, width = hidden.shape
    devices = lax.axis_size("rows")
    chips, hops = devices // 2, devices // 4
    local_experts = w_gate.shape[0]
    chip_experts = 2 * local_experts
    expert_total = local_experts * devices
    order, toward, swap = ring_plan(devices)
    spot = [0] * chips
    for place, chip in enumerate(order):
        spot[chip] = place
    me = lax.axis_index("rows")
    chip, core = me // 2, me % 2
    place = jnp.asarray(spot, jnp.int32)[chip]
    sign = 1 - 2 * core
    core_word = core.astype(jnp.int32).reshape(1)

    def chip_at(offset):
        return jnp.asarray(order, jnp.int32)[(place + sign * offset) % chips]

    def pass_on(array, step):
        return lax.ppermute(array, "rows", toward(step))

    def swapped(array):
        return lax.ppermute(array, "rows", swap)

    weight_other = swapped(out_weight)
    own_experts = (w_gate, w_up, w_down)
    other_experts = tuple(swapped(w) for w in own_experts)

    choice = lax.broadcasted_iota(jnp.int32, (1, 1, expert_total), 2)
    numer = jnp.sum(
        jnp.where(expert_ids[:, :, None] == choice, gate_numer[:, :, None], 0), axis=1
    ).reshape(rows, chips, chip_experts)
    digits = jnp.concatenate([numer // 16, numer % 16], axis=2).astype(BF16)
    extra = -(-2 * chip_experts // 128) * 128
    digits = jnp.pad(digits, ((0, 0), (0, 0), (0, extra - 2 * chip_experts)))

    attended = attend(queries, cache_keys, cache_values, lengths)
    chip_feats = attended.shape[1] // chips
    tokens = jnp.concatenate([attended.reshape(rows, chips, chip_feats), digits], axis=2)
    tokens = tokens.transpose(1, 0, 2)
    got = swapped(jnp.take(tokens, jnp.stack([chip_at(o) for o in range(1, hops)]), axis=0))
    arrived = {}
    for offset in range(hops, 0, -1):
        message = lax.dynamic_index_in_dim(tokens, chip_at(-offset), 0, keepdims=False)
        if offset < hops:
            message = jnp.concatenate([message, got[offset - 1]], axis=0)
        arrived[offset] = pass_on(message, -offset)
    arrived[0] = lax.dynamic_index_in_dim(tokens, chip, 0, keepdims=False)

    partial = {}
    for offset in range(hops, -1, -1):
        partial[offset] = project(core_word, arrived[offset], out_weight, weight_other)

    def ring_sums(partial, message):
        own, other = message, partial[hops - 1][rows:].astype(BF16)
        for offset in range(hops - 1, 0, -1):
            if offset < hops - 1:
                other = (pass_on(other, 1).astype(F32) + partial[offset][rows:]).astype(BF16)
            own = (pass_on(own, 1).astype(F32) + partial[offset][:rows]).astype(BF16)
        other = swapped(pass_on(other, 1)).astype(F32)
        return pass_on(own, 1).astype(F32) + partial[0] + other

    projected = ring_sums(partial, partial[hops].astype(BF16))
    residual = (hidden.astype(F32) + projected).astype(BF16)
    normed = rms_scale(residual.astype(F32), norm_gain).astype(BF16)

    own, other = normed, swapped(normed)
    pieces, bounds = [own], []
    for offset in range(1, hops + 1):
        own = pass_on(own, -1)
        if offset < hops:
            other = pass_on(other, -1)
            pieces = [own, other] + pieces
        else:
            pieces = [own] + pieces

    digits = jnp.concatenate(
        [arrived[offset][:, chip_feats : chip_feats + 2 * chip_experts] for offset in range(hops, -1, -1)],
        axis=0,
    ).astype(F32)
    gates = (digits[:, :chip_experts] * 16.0 + digits[:, chip_experts:]) * gate_scale
    gates = jnp.stack([gates[:, :local_experts], gates[:, local_experts:]], axis=1)
    gates = jnp.where(core == 0, gates, gates[:, ::-1])

    for local in range(local_experts):
        served, far = experts(pieces, gates[:, :, local], own_experts, other_experts, local)
        if local == 0:
            total, first = served, far
        else:
            total = total + served
            first = total[:rows].astype(BF16)

    partial = {0: total[-rows:]}
    for offset in range(1, hops):
        start = rows + (hops - 1 - offset) * 2 * rows
        partial[offset] = total[start : start + 2 * rows]
    combined = ring_sums(partial, first)
    return (residual.astype(F32) + combined).astype(BF16)


def solution(mesh):
    in_specs = (
        P(("groups", "rows"), None),
        P(("groups", "rows"), None, None, None),
        P(("groups", "rows"), None, None, None),
        P(("groups", "rows")),
        P(("groups", "rows"), None),
        P("rows", None),
        P(),
        P("rows", None, None),
        P("rows", None, None),
        P("rows", None, None),
        P(("groups", "rows"), None),
        P(("groups", "rows"), None),
    )
    out_specs = P(("groups", "rows"), None)
    return jax.shard_map(
        on_device, mesh=mesh, in_specs=in_specs, out_specs=out_specs, check_vma=False
    )
```

```python
import functools
import math

import jax
import jax.numpy as jnp
from jax import lax
from jax.experimental import pallas as pl
from jax.experimental.pallas import tpu as pltpu
from jax.sharding import PartitionSpec as P

TOPK = 8
BF16 = jnp.bfloat16
F32 = jnp.float32


gate_scale = 1.0 / 1024.0


def rms_scale(features, norm_gain):
    mean_square = jnp.mean(features * features, axis=-1, keepdims=True)
    return features * lax.rsqrt(mean_square + 1e-06) * norm_gain


def ring_plan(devices):
    chips = devices // 2
    order = list(range(0, chips, 2)) + list(range(chips - 1, 0, -2))
    swap = [(device, device ^ 1) for device in range(devices)]

    def toward(step):
        pairs = []
        for place in range(chips):
            for core in range(2):
                target = order[(place + step * (1 - 2 * core)) % chips]
                pairs.append((2 * order[place] + core, 2 * target + core))
        return pairs

    return order, toward, swap


VMEM = pl.BlockSpec(memory_space=pltpu.VMEM)
SMEM = pl.BlockSpec(memory_space=pltpu.SMEM)


def ring_view(chips):
    me = lax.axis_index("rows")
    chip, core = lax.div(me, 2), lax.rem(me, 2)
    half = lax.div(chip, 2)
    place = jnp.where(lax.rem(chip, 2) == 0, half, chips - 1 - half)

    def chip_at(offset):
        there = lax.rem(place + (1 - 2 * core) * offset + chips, chips)
        return jnp.where(there < chips // 2, 2 * there, 2 * (chips - 1 - there) + 1)

    return chip, core, chip_at


def attend_kernel(
    chips,
    hops,
    chip_experts,
    lengths_ref,
    q_ref,
    k_ref,
    v_ref,
    ids_ref,
    numer_ref,
    far_ref,
    mine_ref,
    give_ref,
    own_ref,
    q_rows,
    out_rows,
    tokens,
):
    step, steps = pl.program_id(0), pl.num_programs(0)
    block, kv_count, cache_len, head_size = k_ref.shape
    rows, feats = q_ref.shape
    heads = feats // head_size
    group = heads // kv_count

    @pl.when(step == 0)
    def _():
        for head in range(heads):
            q_rows[pl.ds(head, rows, stride=heads), :] = q_ref[
                :, head * head_size : (head + 1) * head_size
            ].astype(F32)

    head_of = lax.broadcasted_iota(jnp.int32, (heads, cache_len), 0) // group
    slot = lax.broadcasted_iota(jnp.int32, (heads, cache_len), 1)
    for i in range(block):
        row = step * block + i
        span = pl.ds(pl.multiple_of(row * heads, heads), heads)
        keys = k_ref[i].reshape(kv_count * cache_len, head_size)
        scores = lax.dot_general(
            q_rows[span, :].astype(BF16),
            keys,
            (((1,), (1,)), ((), ())),
            preferred_element_type=F32,
        )
        picked = scores[:, :cache_len]
        for kv in range(1, kv_count):
            picked = jnp.where(
                head_of == kv, scores[:, kv * cache_len : (kv + 1) * cache_len], picked
            )
        picked = picked * (1.0 / math.sqrt(head_size))
        picked = jnp.where(slot < lengths_ref[row], picked, -1e30)
        weights = jnp.exp(picked - jnp.max(picked, axis=1, keepdims=True))
        shares = weights / jnp.sum(weights, axis=1, keepdims=True)
        spread = jnp.concatenate(
            [jnp.where(head_of == kv, shares, 0.0) for kv in range(kv_count)], axis=1
        ).astype(BF16)
        values = v_ref[i].reshape(kv_count * cache_len, head_size)
        out_rows[span, :] = jnp.dot(spread, values, preferred_element_type=F32)

    @pl.when(step == steps - 1)
    def _():
        chip_heads = heads // chips
        chip_feats = chip_heads * head_size
        for head in range(heads):
            start = (head % chip_heads) * head_size
            tokens[head // chip_heads, :, start : start + head_size] = out_rows[
                pl.ds(head, rows, stride=heads), :
            ].astype(BF16)
        extra = tokens.shape[2] - chip_feats
        lane = lax.broadcasted_iota(jnp.int32, (rows, extra), 1)
        expert = jnp.where(lane < chip_experts, lane, lane - chip_experts)
        choices = ids_ref.shape[1]
        named = [jnp.broadcast_to(ids_ref[:, j : j + 1], (rows, extra)) for j in range(choices)]
        numers = [jnp.broadcast_to(numer_ref[:, j : j + 1], (rows, extra)) for j in range(choices)]
        for there in range(chips):
            found = jnp.zeros((rows, extra), jnp.int32)
            for j in range(choices):
                found += jnp.where(named[j] == expert + there * chip_experts, numers[j], 0)
            digit = jnp.where(lane < chip_experts, found >> 4, found & 15)
            digit = jnp.where(lane < 2 * chip_experts, digit, 0)
            tokens[there, :, chip_feats:] = digit.astype(F32).astype(BF16)
        chip, _, chip_at = ring_view(chips)
        far_ref[...] = tokens[chip_at(-hops)]
        own_ref[...] = tokens[chip]
        for offset in range(1, hops):
            mine_ref[offset - 1] = tokens[chip_at(-offset)]
            give_ref[offset - 1] = tokens[chip_at(offset)]


def attend(devices, chip_experts, queries, cache_keys, cache_values, lengths, ids, numer):
    chips, hops = devices // 2, devices // 4
    rows, feats = queries.shape
    kv_count, cache_len, head_size = cache_keys.shape[1:]
    heads = feats // head_size
    extra = -(-2 * chip_experts // 128) * 128
    wide = feats // chips + extra
    block = 8
    cache = pl.BlockSpec((block, kv_count, cache_len, head_size), lambda t: (t, 0, 0, 0))
    one = jax.ShapeDtypeStruct((rows, wide), BF16)
    several = jax.ShapeDtypeStruct((hops - 1, rows, wide), BF16)
    return pl.pallas_call(
        functools.partial(attend_kernel, chips, hops, chip_experts),
        out_shape=(one, several, several, one),
        grid=(rows // block,),
        in_specs=[SMEM, VMEM, cache, cache, VMEM, VMEM],
        out_specs=(VMEM,) * 4,
        scratch_shapes=[
            pltpu.VMEM((rows * heads, head_size), F32),
            pltpu.VMEM((rows * heads, head_size), F32),
            pltpu.VMEM((chips, rows, wide), BF16),
        ],
        compiler_params=pltpu.CompilerParams(vmem_limit_bytes=24 * 1024 * 1024),
        cost_estimate=pl.CostEstimate(
            flops=4 * rows * heads * cache_len * head_size,
            bytes_accessed=4 * rows * kv_count * cache_len * head_size,
            transcendentals=rows * heads * cache_len,
        ),
    )(lengths, queries, cache_keys, cache_values, ids, numer)


def project_kernel(pieces, *refs):
    piece_refs, own_ref, other_ref = refs[:pieces], refs[pieces], refs[pieces + 1]
    out_refs, x_ref = refs[pieces + 2 : -1], refs[-1]
    feats, width = own_ref.shape
    start = 0
    for piece in piece_refs:
        x_ref[start : start + piece.shape[0], :] = piece[:, : 2 * feats]
        start += piece.shape[0]

    def both(first, second):
        tile = 512
        for column in range(0, width, tile):
            done = jnp.dot(
                x_ref[:, :feats], first[:, column : column + tile], preferred_element_type=F32
            ) + jnp.dot(
                x_ref[:, feats:], second[:, column : column + tile], preferred_element_type=F32
            )
            start = 0
            for out in out_refs:
                out[:, column : column + tile] = done[start : start + out.shape[0]].astype(
                    out.dtype
                )
                start += out.shape[0]

    core = lax.rem(lax.axis_index("rows"), 2)

    @pl.when(core == 0)
    def _():
        both(own_ref, other_ref)

    @pl.when(core == 1)
    def _():
        both(other_ref, own_ref)


def project(pieces, kinds, own, other):
    feats, width = own.shape
    rows = sum(piece.shape[0] for piece in pieces)
    return pl.pallas_call(
        functools.partial(project_kernel, len(pieces)),
        out_shape=tuple(
            jax.ShapeDtypeStruct((rows // len(kinds), width), kind) for kind in kinds
        ),
        in_specs=[VMEM] * (len(pieces) + 2),
        out_specs=(VMEM,) * len(kinds),
        scratch_shapes=[pltpu.VMEM((rows, 2 * feats), BF16)],
        compiler_params=pltpu.CompilerParams(vmem_limit_bytes=32 * 1024 * 1024),
        cost_estimate=pl.CostEstimate(
            flops=4 * rows * feats * width, bytes_accessed=4 * feats * width, transcendentals=0
        ),
    )(*pieces, own, other)


def expert_kernel(tiles, hops, local, local_experts, *refs):
    pieces = 2 * hops
    piece_refs, refs = refs[:pieces], refs[pieces:]
    digit_refs, refs = refs[: hops + 1], refs[hops + 1 :]
    own_refs, other_refs, refs = refs[:3], refs[3:6], refs[6:]
    out_refs, (x_ref, gates_ref, inner_ref) = refs[:pieces], refs[pieces:]
    step = pl.program_id(0)
    tile = own_refs[0].shape[2]

    @pl.when(step == 0)
    def _():
        start = 0
        for piece in piece_refs:
            x_ref[start : start + piece.shape[0], :] = piece[...]
            start += piece.shape[0]
        core = lax.rem(lax.axis_index("rows"), 2)
        chip_experts = 2 * local_experts
        start = 0
        for digits in digit_refs:
            feats = digits.shape[1] - 128 * (-(-2 * chip_experts // 128))
            taken = digits[:, feats:].astype(F32)

            def gate(k):
                high, low = taken[:, k : k + 1], taken[:, chip_experts + k : chip_experts + k + 1]
                return (high * 16.0 + low) * gate_scale

            first, second = gate(local), gate(local_experts + local)
            size = digits.shape[0]
            gates_ref[0, start : start + size, :] = jnp.where(core == 0, first, second)
            gates_ref[1, start : start + size, :] = jnp.where(core == 0, second, first)
            start += size

    def raise_up(w_gate, w_up, which):
        gate_proj = jnp.dot(x_ref[...], w_gate[0], preferred_element_type=F32)
        raised = jnp.dot(x_ref[...], w_up[0], preferred_element_type=F32)
        inner = jax.nn.silu(gate_proj) * raised * gates_ref[which]
        span = pl.ds(pl.multiple_of(step * tile, tile), tile)
        inner_ref[:, span] = inner.astype(BF16)

    @pl.when(step < tiles)
    def _():
        raise_up(own_refs[0], own_refs[1], 0)

    @pl.when((step >= tiles) & (step < 2 * tiles))
    def _():
        raise_up(other_refs[0], other_refs[1], 1)

    @pl.when(step >= 2 * tiles)
    def _():
        depth, wide = own_refs[2].shape[1:]
        done = jnp.dot(
            inner_ref[:, :depth], own_refs[2][0], preferred_element_type=F32
        ) + jnp.dot(inner_ref[:, depth:], other_refs[2][0], preferred_element_type=F32)
        span = pl.ds(pl.multiple_of((step - 2 * tiles) * wide, wide), wide)
        start = 0
        for out in out_refs:
            out[:, span] = done[start : start + out.shape[0]].astype(out.dtype)
            start += out.shape[0]


def experts(pieces, kinds, digits, own, other, local):
    local_experts, width, hidden_units = own[0].shape
    rows = sum(piece.shape[0] for piece in pieces)
    tile, wide = 256, 512
    tiles, columns = hidden_units // tile, width // wide

    def specs(turn):
        def place(t):
            return jnp.clip(t - turn * tiles, 0, tiles - 1)

        up = pl.BlockSpec((1, width, tile), lambda t: (local, 0, place(t)))
        down = pl.BlockSpec(
            (1, hidden_units, wide), lambda t: (local, 0, jnp.maximum(t - 2 * tiles, 0))
        )
        return [up, up, down]

    return pl.pallas_call(
        functools.partial(expert_kernel, tiles, len(pieces) // 2, local, local_experts),
        out_shape=tuple(
            jax.ShapeDtypeStruct((piece.shape[0], width), kind)
            for piece, kind in zip(pieces, kinds)
        ),
        grid=(2 * tiles + columns,),
        in_specs=[VMEM] * (len(pieces) + len(digits)) + specs(0) + specs(1),
        out_specs=(VMEM,) * len(pieces),
        scratch_shapes=[
            pltpu.VMEM((rows, width), BF16),
            pltpu.VMEM((2, rows, 1), F32),
            pltpu.VMEM((rows, 2 * hidden_units), BF16),
        ],
        compiler_params=pltpu.CompilerParams(vmem_limit_bytes=48 * 1024 * 1024),
        cost_estimate=pl.CostEstimate(
            flops=12 * rows * hidden_units * width,
            bytes_accessed=12 * hidden_units * width,
            transcendentals=2 * rows * hidden_units,
        ),
    )(*pieces, *digits, *own, *other)


def on_device(
    queries,
    cache_keys,
    cache_values,
    lengths,
    hidden,
    out_weight,
    norm_gain,
    w_gate,
    w_up,
    w_down,
    expert_ids,
    gate_numer,
):
    devices = lax.axis_size("rows")
    hops = devices // 4
    local_experts = w_gate.shape[0]
    order, toward, swap = ring_plan(devices)

    def pass_on(array, step):
        return lax.ppermute(array, "rows", toward(step))

    def swapped(array):
        return lax.ppermute(array, "rows", swap)

    weight_other = swapped(out_weight)
    own_experts = (w_gate, w_up, w_down)
    other_experts = tuple(swapped(w) for w in own_experts)

    far, mine, give, here = attend(
        devices,
        2 * local_experts,
        queries,
        cache_keys,
        cache_values,
        lengths,
        expert_ids,
        gate_numer,
    )
    got = swapped(give)
    arrived = {0: here, hops: pass_on(far, -hops)}
    for offset in range(hops - 1, 0, -1):
        message = jnp.concatenate([mine[offset - 1], got[offset - 1]], axis=0)
        arrived[offset] = pass_on(message, -offset)

    kinds = [BF16, F32, BF16] + [F32] * (2 * hops - 3)
    partial = project([arrived[hops], arrived[hops - 1]], kinds[:3], out_weight, weight_other)
    partial += project(
        [arrived[offset] for offset in range(hops - 2, -1, -1)], kinds[3:], out_weight, weight_other
    )

    def ring_sums(partial):
        own, other = partial[0], partial[2]
        for offset in range(hops - 1, 0, -1):
            spot = 1 + 2 * (hops - 1 - offset)
            if offset < hops - 1:
                other = (pass_on(other, 1).astype(F32) + partial[spot + 1]).astype(BF16)
            own = (pass_on(own, 1).astype(F32) + partial[spot]).astype(BF16)
        other = swapped(pass_on(other, 1)).astype(F32)
        return pass_on(own, 1).astype(F32) + partial[-1] + other

    residual = (hidden.astype(F32) + ring_sums(partial)).astype(BF16)
    normed = rms_scale(residual.astype(F32), norm_gain).astype(BF16)

    own, other = normed, swapped(normed)
    pieces = [own]
    for offset in range(1, hops + 1):
        own = pass_on(own, -1)
        pieces = [own] + pieces
        if offset < hops:
            other = pass_on(other, -1)
            pieces = [own, other] + pieces[1:]

    digits = [arrived[offset] for offset in range(hops, -1, -1)]
    total = None
    for local in range(local_experts):
        plain = [F32] * (2 * hops)
        served = experts(
            pieces,
            kinds if local_experts == 1 else plain,
            digits,
            own_experts,
            other_experts,
            local,
        )
        total = served if local == 0 else [a + b for a, b in zip(total, served)]
    total = [part.astype(kind) for part, kind in zip(total, kinds)]
    return (residual.astype(F32) + ring_sums(total)).astype(BF16)


def solution(mesh):
    in_specs = (
        P(("groups", "rows"), None),
        P(("groups", "rows"), None, None, None),
        P(("groups", "rows"), None, None, None),
        P(("groups", "rows")),
        P(("groups", "rows"), None),
        P("rows", None),
        P(),
        P("rows", None, None),
        P("rows", None, None),
        P("rows", None, None),
        P(("groups", "rows"), None),
        P(("groups", "rows"), None),
    )
    out_specs = P(("groups", "rows"), None)
    return jax.shard_map(
        on_device, mesh=mesh, in_specs=in_specs, out_specs=out_specs, check_vma=False
    )
```

```python
import functools
import math

import jax
import jax.numpy as jnp
from jax import lax
from jax.experimental import pallas as pl
from jax.experimental.pallas import tpu as pltpu
from jax.sharding import PartitionSpec as P

TOPK = 8
BF16 = jnp.bfloat16
F32 = jnp.float32


gate_scale = 1.0 / 1024.0


def rms_scale(features, norm_gain):
    mean_square = jnp.mean(features * features, axis=-1, keepdims=True)
    return features * lax.rsqrt(mean_square + 1e-06) * norm_gain


def ring_plan(devices):
    chips = devices // 2
    order = list(range(0, chips, 2)) + list(range(chips - 1, 0, -2))
    swap = [(device, device ^ 1) for device in range(devices)]

    def toward(step):
        pairs = []
        for place in range(chips):
            for core in range(2):
                target = order[(place + step * (1 - 2 * core)) % chips]
                pairs.append((2 * order[place] + core, 2 * target + core))
        return pairs

    return order, toward, swap


VMEM = pl.BlockSpec(memory_space=pltpu.VMEM)
SMEM = pl.BlockSpec(memory_space=pltpu.SMEM)


def ring_view(chips):
    me = lax.axis_index("rows")
    chip, core = lax.div(me, 2), lax.rem(me, 2)
    half = lax.div(chip, 2)
    place = jnp.where(lax.rem(chip, 2) == 0, half, chips - 1 - half)

    def chip_at(offset):
        there = lax.rem(place + (1 - 2 * core) * offset + chips, chips)
        return jnp.where(there < chips // 2, 2 * there, 2 * (chips - 1 - there) + 1)

    return chip, core, chip_at


def attend_kernel(
    chips,
    hops,
    chip_experts,
    lengths_ref,
    q_ref,
    k_ref,
    v_ref,
    ids_ref,
    numer_ref,
    far_ref,
    mine_ref,
    give_ref,
    own_ref,
    q_rows,
    out_rows,
    tokens,
):
    step, steps = pl.program_id(0), pl.num_programs(0)
    block, kv_count, cache_len, head_size = k_ref.shape
    rows, feats = q_ref.shape
    heads = feats // head_size
    group = heads // kv_count

    @pl.when(step == 0)
    def _():
        for head in range(heads):
            q_rows[pl.ds(head, rows, stride=heads), :] = q_ref[
                :, head * head_size : (head + 1) * head_size
            ].astype(F32)

    head_of = lax.broadcasted_iota(jnp.int32, (block, heads, cache_len), 1) // group
    slot = lax.broadcasted_iota(jnp.int32, (heads, cache_len), 1)
    first = pl.multiple_of(step * block * heads, block * heads)
    asked = q_rows[pl.ds(first, block * heads), :].astype(BF16)
    scores = [
        lax.dot_general(
            asked[i * heads : (i + 1) * heads],
            k_ref[i].reshape(kv_count * cache_len, head_size),
            (((1,), (1,)), ((), ())),
            preferred_element_type=F32,
        )
        for i in range(block)
    ]
    scores = jnp.stack(scores)
    live = jnp.stack([slot < lengths_ref[step * block + i] for i in range(block)])
    picked = scores[:, :, :cache_len]
    for kv in range(1, kv_count):
        picked = jnp.where(
            head_of == kv, scores[:, :, kv * cache_len : (kv + 1) * cache_len], picked
        )
    picked = jnp.where(live, picked * (1.0 / math.sqrt(head_size)), -1e30)
    weights = jnp.exp(picked - jnp.max(picked, axis=2, keepdims=True))
    shares = weights / jnp.sum(weights, axis=2, keepdims=True)
    spread = jnp.concatenate(
        [jnp.where(head_of == kv, shares, 0.0) for kv in range(kv_count)], axis=2
    ).astype(BF16)
    for i in range(block):
        values = v_ref[i].reshape(kv_count * cache_len, head_size)
        out_rows[pl.ds(first + i * heads, heads), :] = jnp.dot(
            spread[i], values, preferred_element_type=F32
        )

    @pl.when(step == steps - 1)
    def _():
        chip_heads = heads // chips
        chip_feats = chip_heads * head_size
        for head in range(heads):
            start = (head % chip_heads) * head_size
            tokens[head // chip_heads, :, start : start + head_size] = out_rows[
                pl.ds(head, rows, stride=heads), :
            ].astype(BF16)
        extra = tokens.shape[2] - chip_feats
        choices = ids_ref.shape[0]
        total = chips * chip_experts
        expert = lax.broadcasted_iota(jnp.int32, (total, rows), 0)
        found = jnp.zeros((total, rows), jnp.int32)
        for j in range(choices):
            found += jnp.where(ids_ref[j : j + 1, :] == expert, numer_ref[j : j + 1, :], 0)
        digits = jnp.concatenate([found >> 4, found & 15], axis=0).astype(F32).astype(BF16)
        source = lax.broadcasted_iota(jnp.int32, (2 * total, extra), 0)
        lane = lax.broadcasted_iota(jnp.int32, (2 * total, extra), 1)
        for there in range(chips):
            base = there * chip_experts
            wanted = jnp.where(lane < chip_experts, base + lane, total + base + lane - chip_experts)
            pick = (source == wanted) & (lane < 2 * chip_experts)
            tokens[there, :, chip_feats:] = lax.dot_general(
                digits,
                jnp.where(pick, 1.0, 0.0).astype(BF16),
                (((0,), (0,)), ((), ())),
                preferred_element_type=F32,
            ).astype(BF16)
        chip, _, chip_at = ring_view(chips)
        far_ref[...] = tokens[chip_at(-hops)]
        own_ref[...] = tokens[chip]
        for offset in range(1, hops):
            mine_ref[offset - 1] = tokens[chip_at(-offset)]
            give_ref[offset - 1] = tokens[chip_at(offset)]


def attend(devices, chip_experts, queries, cache_keys, cache_values, lengths, ids, numer):
    chips, hops = devices // 2, devices // 4
    rows, feats = queries.shape
    kv_count, cache_len, head_size = cache_keys.shape[1:]
    heads = feats // head_size
    extra = -(-2 * chip_experts // 128) * 128
    wide = feats // chips + extra
    block = 16
    cache = pl.BlockSpec((block, kv_count, cache_len, head_size), lambda t: (t, 0, 0, 0))
    one = jax.ShapeDtypeStruct((rows, wide), BF16)
    several = jax.ShapeDtypeStruct((hops - 1, rows, wide), BF16)
    return pl.pallas_call(
        functools.partial(attend_kernel, chips, hops, chip_experts),
        out_shape=(one, several, several, one),
        grid=(rows // block,),
        in_specs=[SMEM, VMEM, cache, cache, VMEM, VMEM],
        out_specs=(VMEM,) * 4,
        scratch_shapes=[
            pltpu.VMEM((rows * heads, head_size), F32),
            pltpu.VMEM((rows * heads, head_size), F32),
            pltpu.VMEM((chips, rows, wide), BF16),
        ],
        compiler_params=pltpu.CompilerParams(vmem_limit_bytes=56 * 1024 * 1024),
        cost_estimate=pl.CostEstimate(
            flops=4 * rows * heads * cache_len * head_size,
            bytes_accessed=4 * rows * kv_count * cache_len * head_size,
            transcendentals=rows * heads * cache_len,
        ),
    )(lengths, queries, cache_keys, cache_values, ids.T, numer.T)


def project_kernel(pieces, *refs):
    piece_refs, own_ref, other_ref = refs[:pieces], refs[pieces], refs[pieces + 1]
    out_refs, x_ref = refs[pieces + 2 : -1], refs[-1]
    feats, width = own_ref.shape
    start = 0
    for piece in piece_refs:
        x_ref[start : start + piece.shape[0], :] = piece[:, : 2 * feats]
        start += piece.shape[0]

    def both(first, second):
        tile = 512
        for column in range(0, width, tile):
            done = jnp.dot(
                x_ref[:, :feats], first[:, column : column + tile], preferred_element_type=F32
            ) + jnp.dot(
                x_ref[:, feats:], second[:, column : column + tile], preferred_element_type=F32
            )
            start = 0
            for out in out_refs:
                out[:, column : column + tile] = done[start : start + out.shape[0]].astype(
                    out.dtype
                )
                start += out.shape[0]

    core = lax.rem(lax.axis_index("rows"), 2)

    @pl.when(core == 0)
    def _():
        both(own_ref, other_ref)

    @pl.when(core == 1)
    def _():
        both(other_ref, own_ref)


def project(pieces, kinds, own, other):
    feats, width = own.shape
    rows = sum(piece.shape[0] for piece in pieces)
    return pl.pallas_call(
        functools.partial(project_kernel, len(pieces)),
        out_shape=tuple(
            jax.ShapeDtypeStruct((rows // len(kinds), width), kind) for kind in kinds
        ),
        in_specs=[VMEM] * (len(pieces) + 2),
        out_specs=(VMEM,) * len(kinds),
        scratch_shapes=[pltpu.VMEM((rows, 2 * feats), BF16)],
        compiler_params=pltpu.CompilerParams(vmem_limit_bytes=32 * 1024 * 1024),
        cost_estimate=pl.CostEstimate(
            flops=4 * rows * feats * width, bytes_accessed=4 * feats * width, transcendentals=0
        ),
    )(*pieces, own, other)


def expert_kernel(tiles, hops, local, local_experts, *refs):
    pieces = 2 * hops
    piece_refs, refs = refs[:pieces], refs[pieces:]
    digit_refs, refs = refs[: hops + 1], refs[hops + 1 :]
    own_refs, other_refs, refs = refs[:3], refs[3:6], refs[6:]
    out_refs, (x_ref, gates_ref, inner_ref) = refs[:pieces], refs[pieces:]
    step = pl.program_id(0)
    tile = own_refs[0].shape[2]

    @pl.when(step == 0)
    def _():
        start = 0
        for piece in piece_refs:
            x_ref[start : start + piece.shape[0], :] = piece[...]
            start += piece.shape[0]
        core = lax.rem(lax.axis_index("rows"), 2)
        chip_experts = 2 * local_experts
        start = 0
        for digits in digit_refs:
            feats = digits.shape[1] - 128 * (-(-2 * chip_experts // 128))
            taken = digits[:, feats:].astype(F32)

            def gate(k):
                high, low = taken[:, k : k + 1], taken[:, chip_experts + k : chip_experts + k + 1]
                return (high * 16.0 + low) * gate_scale

            first, second = gate(local), gate(local_experts + local)
            size = digits.shape[0]
            gates_ref[0, start : start + size, :] = jnp.where(core == 0, first, second)
            gates_ref[1, start : start + size, :] = jnp.where(core == 0, second, first)
            start += size

    def raise_up(w_gate, w_up, which):
        gate_proj = jnp.dot(x_ref[...], w_gate[0], preferred_element_type=F32)
        raised = jnp.dot(x_ref[...], w_up[0], preferred_element_type=F32)
        inner = jax.nn.silu(gate_proj) * raised * gates_ref[which]
        span = pl.ds(pl.multiple_of(step * tile, tile), tile)
        inner_ref[:, span] = inner.astype(BF16)

    @pl.when(step < tiles)
    def _():
        raise_up(own_refs[0], own_refs[1], 0)

    @pl.when((step >= tiles) & (step < 2 * tiles))
    def _():
        raise_up(other_refs[0], other_refs[1], 1)

    @pl.when(step >= 2 * tiles)
    def _():
        depth, wide = own_refs[2].shape[1:]
        done = jnp.dot(
            inner_ref[:, :depth], own_refs[2][0], preferred_element_type=F32
        ) + jnp.dot(inner_ref[:, depth:], other_refs[2][0], preferred_element_type=F32)
        span = pl.ds(pl.multiple_of((step - 2 * tiles) * wide, wide), wide)
        start = 0
        for out in out_refs:
            out[:, span] = done[start : start + out.shape[0]].astype(out.dtype)
            start += out.shape[0]


def experts(pieces, kinds, digits, own, other, local):
    local_experts, width, hidden_units = own[0].shape
    rows = sum(piece.shape[0] for piece in pieces)
    tile, wide = 256, 512
    tiles, columns = hidden_units // tile, width // wide

    def specs(turn):
        def place(t):
            return jnp.clip(t - turn * tiles, 0, tiles - 1)

        up = pl.BlockSpec((1, width, tile), lambda t: (local, 0, place(t)))
        down = pl.BlockSpec(
            (1, hidden_units, wide), lambda t: (local, 0, jnp.maximum(t - 2 * tiles, 0))
        )
        return [up, up, down]

    return pl.pallas_call(
        functools.partial(expert_kernel, tiles, len(pieces) // 2, local, local_experts),
        out_shape=tuple(
            jax.ShapeDtypeStruct((piece.shape[0], width), kind)
            for piece, kind in zip(pieces, kinds)
        ),
        grid=(2 * tiles + columns,),
        in_specs=[VMEM] * (len(pieces) + len(digits)) + specs(0) + specs(1),
        out_specs=(VMEM,) * len(pieces),
        scratch_shapes=[
            pltpu.VMEM((rows, width), BF16),
            pltpu.VMEM((2, rows, 1), F32),
            pltpu.VMEM((rows, 2 * hidden_units), BF16),
        ],
        compiler_params=pltpu.CompilerParams(vmem_limit_bytes=56 * 1024 * 1024),
        cost_estimate=pl.CostEstimate(
            flops=12 * rows * hidden_units * width,
            bytes_accessed=12 * hidden_units * width,
            transcendentals=2 * rows * hidden_units,
        ),
    )(*pieces, *digits, *own, *other)


def on_device(
    queries,
    cache_keys,
    cache_values,
    lengths,
    hidden,
    out_weight,
    norm_gain,
    w_gate,
    w_up,
    w_down,
    expert_ids,
    gate_numer,
):
    devices = lax.axis_size("rows")
    hops = devices // 4
    local_experts = w_gate.shape[0]
    order, toward, swap = ring_plan(devices)

    def pass_on(array, step):
        return lax.ppermute(array, "rows", toward(step))

    def swapped(array):
        return lax.ppermute(array, "rows", swap)

    weight_other = swapped(out_weight)
    own_experts = (w_gate, w_up, w_down)
    other_experts = tuple(swapped(w) for w in own_experts)

    far, mine, give, here = attend(
        devices,
        2 * local_experts,
        queries,
        cache_keys,
        cache_values,
        lengths,
        expert_ids,
        gate_numer,
    )
    got = swapped(give)
    arrived = {0: here, hops: pass_on(far, -hops)}
    for offset in range(hops - 1, 0, -1):
        message = jnp.concatenate([mine[offset - 1], got[offset - 1]], axis=0)
        arrived[offset] = pass_on(message, -offset)

    kinds = [BF16, F32, BF16] + [F32] * (2 * hops - 3)
    partial = project([arrived[hops], arrived[hops - 1]], kinds[:3], out_weight, weight_other)
    partial += project(
        [arrived[offset] for offset in range(hops - 2, -1, -1)], kinds[3:], out_weight, weight_other
    )

    def ring_sums(partial):
        own, other = partial[0], partial[2]
        for offset in range(hops - 1, 0, -1):
            spot = 1 + 2 * (hops - 1 - offset)
            if offset < hops - 1:
                other = (pass_on(other, 1).astype(F32) + partial[spot + 1]).astype(BF16)
            own = (pass_on(own, 1).astype(F32) + partial[spot]).astype(BF16)
        other = swapped(pass_on(other, 1)).astype(F32)
        return pass_on(own, 1).astype(F32) + partial[-1] + other

    residual = (hidden.astype(F32) + ring_sums(partial)).astype(BF16)
    normed = rms_scale(residual.astype(F32), norm_gain).astype(BF16)

    own, other = normed, swapped(normed)
    pieces = [own]
    for offset in range(1, hops + 1):
        own = pass_on(own, -1)
        pieces = [own] + pieces
        if offset < hops:
            other = pass_on(other, -1)
            pieces = [own, other] + pieces[1:]

    digits = [arrived[offset] for offset in range(hops, -1, -1)]
    total = None
    for local in range(local_experts):
        plain = [F32] * (2 * hops)
        served = experts(
            pieces,
            kinds if local_experts == 1 else plain,
            digits,
            own_experts,
            other_experts,
            local,
        )
        total = served if local == 0 else [a + b for a, b in zip(total, served)]
    total = [part.astype(kind) for part, kind in zip(total, kinds)]
    return (residual.astype(F32) + ring_sums(total)).astype(BF16)


def solution(mesh):
    in_specs = (
        P(("groups", "rows"), None),
        P(("groups", "rows"), None, None, None),
        P(("groups", "rows"), None, None, None),
        P(("groups", "rows")),
        P(("groups", "rows"), None),
        P("rows", None),
        P(),
        P("rows", None, None),
        P("rows", None, None),
        P("rows", None, None),
        P(("groups", "rows"), None),
        P(("groups", "rows"), None),
    )
    out_specs = P(("groups", "rows"), None)
    return jax.shard_map(
        on_device, mesh=mesh, in_specs=in_specs, out_specs=out_specs, check_vma=False
    )
```

```python
import functools
import math

import jax
import jax.numpy as jnp
from jax import lax
from jax.experimental import pallas as pl
from jax.experimental.pallas import tpu as pltpu
from jax.sharding import PartitionSpec as P

TOPK = 8
BF16 = jnp.bfloat16
F32 = jnp.float32


gate_scale = 1.0 / 1024.0


def rms_scale(features, norm_gain):
    mean_square = jnp.mean(features * features, axis=-1, keepdims=True)
    return features * lax.rsqrt(mean_square + 1e-06) * norm_gain


def ring_plan(devices):
    chips = devices // 2
    order = list(range(0, chips, 2)) + list(range(chips - 1, 0, -2))
    swap = [(device, device ^ 1) for device in range(devices)]

    def toward(step):
        pairs = []
        for place in range(chips):
            for core in range(2):
                target = order[(place + step * (1 - 2 * core)) % chips]
                pairs.append((2 * order[place] + core, 2 * target + core))
        return pairs

    return order, toward, swap


VMEM = pl.BlockSpec(memory_space=pltpu.VMEM)
SMEM = pl.BlockSpec(memory_space=pltpu.SMEM)


def ring_view(chips):
    me = lax.axis_index("rows")
    chip, core = lax.div(me, 2), lax.rem(me, 2)
    half = lax.div(chip, 2)
    place = jnp.where(lax.rem(chip, 2) == 0, half, chips - 1 - half)

    def chip_at(offset):
        there = lax.rem(place + (1 - 2 * core) * offset + chips, chips)
        return jnp.where(there < chips // 2, 2 * there, 2 * (chips - 1 - there) + 1)

    return chip, core, chip_at


def attend_kernel(
    chips,
    hops,
    chip_experts,
    lengths_ref,
    q_ref,
    k_ref,
    v_ref,
    ids_ref,
    numer_ref,
    far_ref,
    mine_ref,
    give_ref,
    own_ref,
    q_rows,
    out_rows,
    tokens,
):
    step, steps = pl.program_id(0), pl.num_programs(0)
    block, kv_count, cache_len, head_size = k_ref.shape
    rows, feats = q_ref.shape
    heads = feats // head_size
    group = heads // kv_count

    @pl.when(step == 0)
    def _():
        for head in range(heads):
            q_rows[pl.ds(head, rows, stride=heads), :] = q_ref[
                :, head * head_size : (head + 1) * head_size
            ].astype(F32)

    head_of = lax.broadcasted_iota(jnp.int32, (block, heads, cache_len), 1) // group
    slot = lax.broadcasted_iota(jnp.int32, (heads, cache_len), 1)
    first = pl.multiple_of(step * block * heads, block * heads)
    asked = q_rows[pl.ds(first, block * heads), :].astype(BF16)
    scores = [
        lax.dot_general(
            asked[i * heads : (i + 1) * heads],
            k_ref[i].reshape(kv_count * cache_len, head_size),
            (((1,), (1,)), ((), ())),
            preferred_element_type=F32,
        )
        for i in range(block)
    ]
    scores = jnp.stack(scores)
    live = jnp.stack([slot < lengths_ref[step * block + i] for i in range(block)])
    picked = scores[:, :, :cache_len]
    for kv in range(1, kv_count):
        picked = jnp.where(
            head_of == kv, scores[:, :, kv * cache_len : (kv + 1) * cache_len], picked
        )
    picked = jnp.where(live, picked * (1.0 / math.sqrt(head_size)), -1e30)
    weights = jnp.exp(picked - jnp.max(picked, axis=2, keepdims=True))
    shares = weights / jnp.sum(weights, axis=2, keepdims=True)
    spread = jnp.concatenate(
        [jnp.where(head_of == kv, shares, 0.0) for kv in range(kv_count)], axis=2
    ).astype(BF16)
    for i in range(block):
        values = v_ref[i].reshape(kv_count * cache_len, head_size)
        out_rows[pl.ds(first + i * heads, heads), :] = jnp.dot(
            spread[i], values, preferred_element_type=F32
        )

    @pl.when(step == steps - 1)
    def _():
        chip_heads = heads // chips
        chip_feats = chip_heads * head_size
        for head in range(heads):
            start = (head % chip_heads) * head_size
            tokens[head // chip_heads, :, start : start + head_size] = out_rows[
                pl.ds(head, rows, stride=heads), :
            ].astype(BF16)
        extra = tokens.shape[2] - chip_feats
        choices = ids_ref.shape[0]
        total = chips * chip_experts
        expert = lax.broadcasted_iota(jnp.int32, (total, rows), 0)
        found = jnp.zeros((total, rows), jnp.int32)
        for j in range(choices):
            found += jnp.where(ids_ref[j : j + 1, :] == expert, numer_ref[j : j + 1, :], 0)
        digits = jnp.concatenate([found >> 4, found & 15], axis=0).astype(F32).astype(BF16)
        source = lax.broadcasted_iota(jnp.int32, (2 * total, extra), 0)
        lane = lax.broadcasted_iota(jnp.int32, (2 * total, extra), 1)
        for there in range(chips):
            base = there * chip_experts
            wanted = jnp.where(lane < chip_experts, base + lane, total + base + lane - chip_experts)
            pick = (source == wanted) & (lane < 2 * chip_experts)
            tokens[there, :, chip_feats:] = lax.dot_general(
                digits,
                jnp.where(pick, 1.0, 0.0).astype(BF16),
                (((0,), (0,)), ((), ())),
                preferred_element_type=F32,
            ).astype(BF16)
        chip, _, chip_at = ring_view(chips)
        far_ref[...] = tokens[chip_at(-hops)]
        own_ref[...] = tokens[chip]
        for offset in range(1, hops):
            mine_ref[offset - 1] = tokens[chip_at(-offset)]
            give_ref[offset - 1] = tokens[chip_at(offset)]


def attend(devices, chip_experts, queries, cache_keys, cache_values, lengths, ids, numer):
    chips, hops = devices // 2, devices // 4
    rows, feats = queries.shape
    kv_count, cache_len, head_size = cache_keys.shape[1:]
    heads = feats // head_size
    extra = -(-2 * chip_experts // 128) * 128
    wide = feats // chips + extra
    block = 16
    cache = pl.BlockSpec((block, kv_count, cache_len, head_size), lambda t: (t, 0, 0, 0))
    one = jax.ShapeDtypeStruct((rows, wide), BF16)
    several = jax.ShapeDtypeStruct((hops - 1, rows, wide), BF16)
    return pl.pallas_call(
        functools.partial(attend_kernel, chips, hops, chip_experts),
        out_shape=(one, several, several, one),
        grid=(rows // block,),
        in_specs=[SMEM, VMEM, cache, cache, VMEM, VMEM],
        out_specs=(VMEM,) * 4,
        scratch_shapes=[
            pltpu.VMEM((rows * heads, head_size), F32),
            pltpu.VMEM((rows * heads, head_size), F32),
            pltpu.VMEM((chips, rows, wide), BF16),
        ],
        compiler_params=pltpu.CompilerParams(vmem_limit_bytes=56 * 1024 * 1024),
        cost_estimate=pl.CostEstimate(
            flops=4 * rows * heads * cache_len * head_size,
            bytes_accessed=4 * rows * kv_count * cache_len * head_size,
            transcendentals=rows * heads * cache_len,
        ),
    )(lengths, queries, cache_keys, cache_values, ids.T, numer.T)


def project_kernel(pieces, *refs):
    piece_refs, own_ref, other_ref = refs[:pieces], refs[pieces], refs[pieces + 1]
    out_refs, x_ref = refs[pieces + 2 : -1], refs[-1]
    feats, width = own_ref.shape
    start = 0
    for piece in piece_refs:
        x_ref[start : start + piece.shape[0], :] = piece[:, : 2 * feats]
        start += piece.shape[0]

    def both(first, second):
        tile = 512
        for column in range(0, width, tile):
            done = jnp.dot(
                x_ref[:, :feats], first[:, column : column + tile], preferred_element_type=F32
            ) + jnp.dot(
                x_ref[:, feats:], second[:, column : column + tile], preferred_element_type=F32
            )
            start = 0
            for out in out_refs:
                out[:, column : column + tile] = done[start : start + out.shape[0]].astype(
                    out.dtype
                )
                start += out.shape[0]

    core = lax.rem(lax.axis_index("rows"), 2)

    @pl.when(core == 0)
    def _():
        both(own_ref, other_ref)

    @pl.when(core == 1)
    def _():
        both(other_ref, own_ref)


def project(pieces, kinds, own, other):
    feats, width = own.shape
    rows = sum(piece.shape[0] for piece in pieces)
    return pl.pallas_call(
        functools.partial(project_kernel, len(pieces)),
        out_shape=tuple(
            jax.ShapeDtypeStruct((rows // len(kinds), width), kind) for kind in kinds
        ),
        in_specs=[VMEM] * (len(pieces) + 2),
        out_specs=(VMEM,) * len(kinds),
        scratch_shapes=[pltpu.VMEM((rows, 2 * feats), BF16)],
        compiler_params=pltpu.CompilerParams(vmem_limit_bytes=32 * 1024 * 1024),
        cost_estimate=pl.CostEstimate(
            flops=4 * rows * feats * width, bytes_accessed=4 * feats * width, transcendentals=0
        ),
    )(*pieces, own, other)


def expert_kernel(pieces, local, local_experts, *refs):
    piece_refs, digits_ref, refs = refs[:pieces], refs[pieces], refs[pieces + 1 :]
    weight_refs, refs = refs[:6], refs[6:]
    out_refs, (x_ref, inner_ref) = refs[:pieces], refs[pieces:]
    size = piece_refs[0].shape[0]
    for index, piece in enumerate(piece_refs):
        x_ref[index * size : (index + 1) * size, :] = piece[...]
    core = lax.rem(lax.axis_index("rows"), 2)
    chip_experts = 2 * local_experts
    feats = digits_ref.shape[1] - 128 * (-(-2 * chip_experts // 128))
    taken = digits_ref[:, feats:].astype(F32)

    def gate(k):
        high, low = taken[:, k : k + 1], taken[:, chip_experts + k : chip_experts + k + 1]
        return (high * 16.0 + low) * gate_scale

    first, second = gate(local), gate(local_experts + local)
    gates = (jnp.where(core == 0, first, second), jnp.where(core == 0, second, first))
    hidden_units, width = weight_refs[2].shape[1:]
    tile = 256
    for which in range(2):
        w_gate, w_up = weight_refs[3 * which], weight_refs[3 * which + 1]
        for start in range(0, hidden_units, tile):
            gate_proj = jnp.dot(
                x_ref[...], w_gate[local, :, start : start + tile], preferred_element_type=F32
            )
            raised = jnp.dot(
                x_ref[...], w_up[local, :, start : start + tile], preferred_element_type=F32
            )
            inner = jax.nn.silu(gate_proj) * raised * gates[which]
            place = which * hidden_units + start
            inner_ref[:, place : place + tile] = inner.astype(BF16)
    tile = 512
    for start in range(0, width, tile):
        done = jnp.dot(
            inner_ref[:, :hidden_units],
            weight_refs[2][local, :, start : start + tile],
            preferred_element_type=F32,
        ) + jnp.dot(
            inner_ref[:, hidden_units:],
            weight_refs[5][local, :, start : start + tile],
            preferred_element_type=F32,
        )
        for index, out in enumerate(out_refs):
            out[:, start : start + tile] = done[index * size : (index + 1) * size].astype(
                out.dtype
            )


def experts(pieces, kinds, digits, own, other, local):
    local_experts, width, hidden_units = own[0].shape
    rows = sum(piece.shape[0] for piece in pieces)
    return pl.pallas_call(
        functools.partial(expert_kernel, len(pieces), local, local_experts),
        out_shape=tuple(
            jax.ShapeDtypeStruct((piece.shape[0], width), kind)
            for piece, kind in zip(pieces, kinds)
        ),
        in_specs=[VMEM] * (len(pieces) + 7),
        out_specs=(VMEM,) * len(pieces),
        scratch_shapes=[
            pltpu.VMEM((rows, width), BF16),
            pltpu.VMEM((rows, 2 * hidden_units), BF16),
        ],
        compiler_params=pltpu.CompilerParams(vmem_limit_bytes=16 * 1024 * 1024),
        cost_estimate=pl.CostEstimate(
            flops=24 * rows * hidden_units * width,
            bytes_accessed=rows * width,
            transcendentals=2 * rows * hidden_units,
        ),
    )(*pieces, digits, *own, *other)


def on_device(
    queries,
    cache_keys,
    cache_values,
    lengths,
    hidden,
    out_weight,
    norm_gain,
    w_gate,
    w_up,
    w_down,
    expert_ids,
    gate_numer,
):
    devices = lax.axis_size("rows")
    hops = devices // 4
    local_experts = w_gate.shape[0]
    order, toward, swap = ring_plan(devices)

    def pass_on(array, step):
        return lax.ppermute(array, "rows", toward(step))

    def swapped(array):
        return lax.ppermute(array, "rows", swap)

    weight_other = swapped(out_weight)
    own_experts = (w_gate, w_up, w_down)
    other_experts = tuple(swapped(w) for w in own_experts)

    far, mine, give, here = attend(
        devices,
        2 * local_experts,
        queries,
        cache_keys,
        cache_values,
        lengths,
        expert_ids,
        gate_numer,
    )
    got = swapped(give)
    arrived = {0: here, hops: pass_on(far, -hops)}
    for offset in range(hops - 1, 0, -1):
        message = jnp.concatenate([mine[offset - 1], got[offset - 1]], axis=0)
        arrived[offset] = pass_on(message, -offset)

    kinds = [BF16, F32, BF16] + [F32] * (2 * hops - 3)
    partial = project([arrived[hops], arrived[hops - 1]], kinds[:3], out_weight, weight_other)
    partial += project(
        [arrived[offset] for offset in range(hops - 2, -1, -1)], kinds[3:], out_weight, weight_other
    )

    def ring_sums(partial):
        own, other = partial[0], partial[2]
        for offset in range(hops - 1, 0, -1):
            spot = 1 + 2 * (hops - 1 - offset)
            if offset < hops - 1:
                other = (pass_on(other, 1).astype(F32) + partial[spot + 1]).astype(BF16)
            own = (pass_on(own, 1).astype(F32) + partial[spot]).astype(BF16)
        other = swapped(pass_on(other, 1)).astype(F32)
        return pass_on(own, 1).astype(F32) + partial[-1] + other

    residual = (hidden.astype(F32) + ring_sums(partial)).astype(BF16)
    normed = rms_scale(residual.astype(F32), norm_gain).astype(BF16)

    def serve(pieces, kinds, digits):
        total = None
        for local in range(local_experts):
            plain = kinds if local_experts == 1 else [F32] * len(kinds)
            served = experts(pieces, plain, digits, own_experts, other_experts, local)
            total = served if local == 0 else [a + b for a, b in zip(total, served)]
        return [part.astype(kind) for part, kind in zip(total, kinds)]

    own, other = normed, swapped(normed)
    total = serve([own], [F32], arrived[0])
    for offset in range(1, hops):
        own, other = pass_on(own, -1), pass_on(other, -1)
        kinds = [F32, BF16 if offset == hops - 1 else F32]
        total = serve([own, other], kinds, arrived[offset]) + total
    total = serve([pass_on(own, -1)], [BF16], arrived[hops]) + total
    return (residual.astype(F32) + ring_sums(total)).astype(BF16)


def solution(mesh):
    in_specs = (
        P(("groups", "rows"), None),
        P(("groups", "rows"), None, None, None),
        P(("groups", "rows"), None, None, None),
        P(("groups", "rows")),
        P(("groups", "rows"), None),
        P("rows", None),
        P(),
        P("rows", None, None),
        P("rows", None, None),
        P("rows", None, None),
        P(("groups", "rows"), None),
        P(("groups", "rows"), None),
    )
    out_specs = P(("groups", "rows"), None)
    return jax.shard_map(
        on_device, mesh=mesh, in_specs=in_specs, out_specs=out_specs, check_vma=False
    )
```

```python
import functools
import math

import jax
import jax.numpy as jnp
from jax import lax
from jax.experimental import pallas as pl
from jax.experimental.pallas import tpu as pltpu
from jax.sharding import PartitionSpec as P

TOPK = 8
BF16 = jnp.bfloat16
F32 = jnp.float32


gate_scale = 1.0 / 1024.0


def rms_scale(features, norm_gain):
    mean_square = jnp.mean(features * features, axis=-1, keepdims=True)
    return features * lax.rsqrt(mean_square + 1e-06) * norm_gain


def ring_plan(devices):
    chips = devices // 2
    order = list(range(0, chips, 2)) + list(range(chips - 1, 0, -2))
    swap = [(device, device ^ 1) for device in range(devices)]

    def toward(step):
        pairs = []
        for place in range(chips):
            for core in range(2):
                target = order[(place + step * (1 - 2 * core)) % chips]
                pairs.append((2 * order[place] + core, 2 * target + core))
        return pairs

    return order, toward, swap


VMEM = pl.BlockSpec(memory_space=pltpu.VMEM)
SMEM = pl.BlockSpec(memory_space=pltpu.SMEM)


def ring_view(chips):
    me = lax.axis_index("rows")
    chip, core = lax.div(me, 2), lax.rem(me, 2)
    half = lax.div(chip, 2)
    place = jnp.where(lax.rem(chip, 2) == 0, half, chips - 1 - half)

    def chip_at(offset):
        there = lax.rem(place + (1 - 2 * core) * offset + chips, chips)
        return jnp.where(there < chips // 2, 2 * there, 2 * (chips - 1 - there) + 1)

    return chip, core, chip_at


def attend_kernel(
    chips,
    hops,
    chip_experts,
    lengths_ref,
    q_ref,
    k_ref,
    v_ref,
    ids_ref,
    numer_ref,
    far_ref,
    mine_ref,
    give_ref,
    own_ref,
    q_rows,
    out_rows,
    tokens,
):
    step, steps = pl.program_id(0), pl.num_programs(0)
    block, kv_count, cache_len, head_size = k_ref.shape
    rows, feats = q_ref.shape
    heads = feats // head_size
    group = heads // kv_count

    @pl.when(step == 0)
    def _():
        for head in range(heads):
            q_rows[pl.ds(head, rows, stride=heads), :] = q_ref[
                :, head * head_size : (head + 1) * head_size
            ].astype(F32)

    head_of = lax.broadcasted_iota(jnp.int32, (block, heads, cache_len), 1) // group
    slot = lax.broadcasted_iota(jnp.int32, (heads, cache_len), 1)
    first = pl.multiple_of(step * block * heads, block * heads)
    asked = q_rows[pl.ds(first, block * heads), :].astype(BF16)
    scores = [
        lax.dot_general(
            asked[i * heads : (i + 1) * heads],
            k_ref[i].reshape(kv_count * cache_len, head_size),
            (((1,), (1,)), ((), ())),
            preferred_element_type=F32,
        )
        for i in range(block)
    ]
    scores = jnp.stack(scores)
    live = jnp.stack([slot < lengths_ref[step * block + i] for i in range(block)])
    picked = scores[:, :, :cache_len]
    for kv in range(1, kv_count):
        picked = jnp.where(
            head_of == kv, scores[:, :, kv * cache_len : (kv + 1) * cache_len], picked
        )
    picked = jnp.where(live, picked * (1.0 / math.sqrt(head_size)), -1e30)
    weights = jnp.exp(picked - jnp.max(picked, axis=2, keepdims=True))
    shares = weights / jnp.sum(weights, axis=2, keepdims=True)
    spread = jnp.concatenate(
        [jnp.where(head_of == kv, shares, 0.0) for kv in range(kv_count)], axis=2
    ).astype(BF16)
    for i in range(block):
        values = v_ref[i].reshape(kv_count * cache_len, head_size)
        out_rows[pl.ds(first + i * heads, heads), :] = jnp.dot(
            spread[i], values, preferred_element_type=F32
        )

    @pl.when(step == steps - 1)
    def _():
        chip_heads = heads // chips
        chip_feats = chip_heads * head_size
        for head in range(heads):
            start = (head % chip_heads) * head_size
            tokens[head // chip_heads, :, start : start + head_size] = out_rows[
                pl.ds(head, rows, stride=heads), :
            ].astype(BF16)
        extra = tokens.shape[2] - chip_feats
        choices = ids_ref.shape[0]
        total = chips * chip_experts
        expert = lax.broadcasted_iota(jnp.int32, (total, rows), 0)
        found = jnp.zeros((total, rows), jnp.int32)
        for j in range(choices):
            found += jnp.where(ids_ref[j : j + 1, :] == expert, numer_ref[j : j + 1, :], 0)
        digits = jnp.concatenate([found >> 4, found & 15], axis=0).astype(F32).astype(BF16)
        source = lax.broadcasted_iota(jnp.int32, (2 * total, extra), 0)
        lane = lax.broadcasted_iota(jnp.int32, (2 * total, extra), 1)
        for there in range(chips):
            base = there * chip_experts
            wanted = jnp.where(lane < chip_experts, base + lane, total + base + lane - chip_experts)
            pick = (source == wanted) & (lane < 2 * chip_experts)
            tokens[there, :, chip_feats:] = lax.dot_general(
                digits,
                jnp.where(pick, 1.0, 0.0).astype(BF16),
                (((0,), (0,)), ((), ())),
                preferred_element_type=F32,
            ).astype(BF16)
        chip, _, chip_at = ring_view(chips)
        far_ref[...] = tokens[chip_at(-hops)]
        own_ref[...] = tokens[chip]
        for offset in range(1, hops):
            mine_ref[offset - 1] = tokens[chip_at(-offset)]
            give_ref[offset - 1] = tokens[chip_at(offset)]


def attend(devices, chip_experts, queries, cache_keys, cache_values, lengths, ids, numer):
    chips, hops = devices // 2, devices // 4
    rows, feats = queries.shape
    kv_count, cache_len, head_size = cache_keys.shape[1:]
    heads = feats // head_size
    extra = -(-2 * chip_experts // 128) * 128
    wide = feats // chips + extra
    block = 16
    cache = pl.BlockSpec((block, kv_count, cache_len, head_size), lambda t: (t, 0, 0, 0))
    one = jax.ShapeDtypeStruct((rows, wide), BF16)
    several = jax.ShapeDtypeStruct((hops - 1, rows, wide), BF16)
    return pl.pallas_call(
        functools.partial(attend_kernel, chips, hops, chip_experts),
        out_shape=(one, several, several, one),
        grid=(rows // block,),
        in_specs=[SMEM, VMEM, cache, cache, VMEM, VMEM],
        out_specs=(VMEM,) * 4,
        scratch_shapes=[
            pltpu.VMEM((rows * heads, head_size), F32),
            pltpu.VMEM((rows * heads, head_size), F32),
            pltpu.VMEM((chips, rows, wide), BF16),
        ],
        compiler_params=pltpu.CompilerParams(vmem_limit_bytes=54 * 1024 * 1024),
        cost_estimate=pl.CostEstimate(
            flops=4 * rows * heads * cache_len * head_size,
            bytes_accessed=4 * rows * kv_count * cache_len * head_size,
            transcendentals=rows * heads * cache_len,
        ),
    )(lengths, queries, cache_keys, cache_values, ids.T, numer.T)


def project_kernel(pieces, *refs):
    piece_refs, own_ref, other_ref = refs[:pieces], refs[pieces], refs[pieces + 1]
    out_refs, x_ref = refs[pieces + 2 : -1], refs[-1]
    feats, width = own_ref.shape
    start = 0
    for piece in piece_refs:
        x_ref[start : start + piece.shape[0], :] = piece[:, : 2 * feats]
        start += piece.shape[0]

    def both(first, second):
        tile = 512
        for column in range(0, width, tile):
            done = jnp.dot(
                x_ref[:, :feats], first[:, column : column + tile], preferred_element_type=F32
            ) + jnp.dot(
                x_ref[:, feats:], second[:, column : column + tile], preferred_element_type=F32
            )
            start = 0
            for out in out_refs:
                out[:, column : column + tile] = done[start : start + out.shape[0]].astype(
                    out.dtype
                )
                start += out.shape[0]

    core = lax.rem(lax.axis_index("rows"), 2)

    @pl.when(core == 0)
    def _():
        both(own_ref, other_ref)

    @pl.when(core == 1)
    def _():
        both(other_ref, own_ref)


def project(pieces, kinds, own, other):
    feats, width = own.shape
    rows = sum(piece.shape[0] for piece in pieces)
    return pl.pallas_call(
        functools.partial(project_kernel, len(pieces)),
        out_shape=tuple(
            jax.ShapeDtypeStruct((rows // len(kinds), width), kind) for kind in kinds
        ),
        in_specs=[VMEM] * (len(pieces) + 2),
        out_specs=(VMEM,) * len(kinds),
        scratch_shapes=[pltpu.VMEM((rows, 2 * feats), BF16)],
        compiler_params=pltpu.CompilerParams(vmem_limit_bytes=32 * 1024 * 1024),
        cost_estimate=pl.CostEstimate(
            flops=4 * rows * feats * width, bytes_accessed=4 * feats * width, transcendentals=0
        ),
    )(*pieces, own, other)


def expert_kernel(pieces, blocks, local, local_experts, *refs):
    piece_refs, digit_refs, refs = refs[:pieces], refs[pieces : pieces + blocks], refs[pieces + blocks :]
    weight_refs, refs = refs[:6], refs[6:]
    out_refs, (x_ref, inner_ref, gates_ref) = refs[:pieces], refs[pieces:]
    size = piece_refs[0].shape[0]
    for index, piece in enumerate(piece_refs):
        x_ref[index * size : (index + 1) * size, :] = piece[...]
    core = lax.rem(lax.axis_index("rows"), 2)
    chip_experts = 2 * local_experts
    start = 0
    for digits in digit_refs:
        feats = digits.shape[1] - 128 * (-(-2 * chip_experts // 128))
        taken = digits[:, feats:].astype(F32)

        def gate(k):
            high, low = taken[:, k : k + 1], taken[:, chip_experts + k : chip_experts + k + 1]
            return (high * 16.0 + low) * gate_scale

        first, second = gate(local), gate(local_experts + local)
        stop = start + digits.shape[0]
        gates_ref[0, start:stop, :] = jnp.where(core == 0, first, second)
        gates_ref[1, start:stop, :] = jnp.where(core == 0, second, first)
        start = stop
    gates = (gates_ref[0], gates_ref[1])
    hidden_units, width = weight_refs[2].shape[1:]
    tile = 256
    for which in range(2):
        w_gate, w_up = weight_refs[3 * which], weight_refs[3 * which + 1]
        for start in range(0, hidden_units, tile):
            gate_proj = jnp.dot(
                x_ref[...], w_gate[local, :, start : start + tile], preferred_element_type=F32
            )
            raised = jnp.dot(
                x_ref[...], w_up[local, :, start : start + tile], preferred_element_type=F32
            )
            inner = jax.nn.silu(gate_proj) * raised * gates[which]
            place = which * hidden_units + start
            inner_ref[:, place : place + tile] = inner.astype(BF16)
    tile = 512
    for start in range(0, width, tile):
        done = jnp.dot(
            inner_ref[:, :hidden_units],
            weight_refs[2][local, :, start : start + tile],
            preferred_element_type=F32,
        ) + jnp.dot(
            inner_ref[:, hidden_units:],
            weight_refs[5][local, :, start : start + tile],
            preferred_element_type=F32,
        )
        for index, out in enumerate(out_refs):
            out[:, start : start + tile] = done[index * size : (index + 1) * size].astype(
                out.dtype
            )


def experts(pieces, kinds, digits, own, other, local):
    local_experts, width, hidden_units = own[0].shape
    rows = sum(piece.shape[0] for piece in pieces)
    return pl.pallas_call(
        functools.partial(expert_kernel, len(pieces), len(digits), local, local_experts),
        out_shape=tuple(
            jax.ShapeDtypeStruct((piece.shape[0], width), kind)
            for piece, kind in zip(pieces, kinds)
        ),
        in_specs=[VMEM] * (len(pieces) + len(digits) + 6),
        out_specs=(VMEM,) * len(pieces),
        scratch_shapes=[
            pltpu.VMEM((rows, width), BF16),
            pltpu.VMEM((rows, 2 * hidden_units), BF16),
            pltpu.VMEM((2, rows, 1), F32),
        ],
        compiler_params=pltpu.CompilerParams(vmem_limit_bytes=16 * 1024 * 1024),
        cost_estimate=pl.CostEstimate(
            flops=12 * rows * hidden_units * width,
            bytes_accessed=rows * width,
            transcendentals=2 * rows * hidden_units,
        ),
    )(*pieces, *digits, *own, *other)


def on_device(
    queries,
    cache_keys,
    cache_values,
    lengths,
    hidden,
    out_weight,
    norm_gain,
    w_gate,
    w_up,
    w_down,
    expert_ids,
    gate_numer,
):
    devices = lax.axis_size("rows")
    hops = devices // 4
    local_experts = w_gate.shape[0]
    order, toward, swap = ring_plan(devices)

    def pass_on(array, step):
        return lax.ppermute(array, "rows", toward(step))

    def swapped(array):
        return lax.ppermute(array, "rows", swap)

    weight_other = swapped(out_weight)
    own_experts = (w_gate, w_up, w_down)
    other_experts = tuple(swapped(w) for w in own_experts)

    far, mine, give, here = attend(
        devices,
        2 * local_experts,
        queries,
        cache_keys,
        cache_values,
        lengths,
        expert_ids,
        gate_numer,
    )
    got = swapped(give)
    arrived = {0: here, hops: pass_on(far, -hops)}
    for offset in range(hops - 1, 0, -1):
        message = jnp.concatenate([mine[offset - 1], got[offset - 1]], axis=0)
        arrived[offset] = pass_on(message, -offset)

    kinds = [BF16, F32, BF16] + [F32] * (2 * hops - 3)
    partial = project([arrived[hops], arrived[hops - 1]], kinds[:3], out_weight, weight_other)
    partial += project(
        [arrived[offset] for offset in range(hops - 2, -1, -1)], kinds[3:], out_weight, weight_other
    )

    def ring_sums(partial):
        own, other = partial[0], partial[2]
        for offset in range(hops - 1, 0, -1):
            spot = 1 + 2 * (hops - 1 - offset)
            if offset < hops - 1:
                other = (pass_on(other, 1).astype(F32) + partial[spot + 1]).astype(BF16)
            own = (pass_on(own, 1).astype(F32) + partial[spot]).astype(BF16)
        other = swapped(pass_on(other, 1)).astype(F32)
        return pass_on(own, 1).astype(F32) + partial[-1] + other

    residual = (hidden.astype(F32) + ring_sums(partial)).astype(BF16)
    normed = rms_scale(residual.astype(F32), norm_gain).astype(BF16)

    def serve(pieces, kinds, digits):
        total = None
        for local in range(local_experts):
            plain = kinds if local_experts == 1 else [F32] * len(kinds)
            served = experts(pieces, plain, digits, own_experts, other_experts, local)
            total = served if local == 0 else [a + b for a, b in zip(total, served)]
        return [part.astype(kind) for part, kind in zip(total, kinds)]

    own, other = normed, swapped(normed)
    pieces = [own]
    for offset in range(1, hops):
        own, other = pass_on(own, -1), pass_on(other, -1)
        pieces = [own, other] + pieces
    pieces = [pass_on(own, -1)] + pieces
    digits = [arrived[offset] for offset in range(hops, -1, -1)]
    total = serve(pieces[:3], kinds[:3], digits[:2]) + serve(pieces[3:], kinds[3:], digits[2:])
    return (residual.astype(F32) + ring_sums(total)).astype(BF16)


def solution(mesh):
    in_specs = (
        P(("groups", "rows"), None),
        P(("groups", "rows"), None, None, None),
        P(("groups", "rows"), None, None, None),
        P(("groups", "rows")),
        P(("groups", "rows"), None),
        P("rows", None),
        P(),
        P("rows", None, None),
        P("rows", None, None),
        P("rows", None, None),
        P(("groups", "rows"), None),
        P(("groups", "rows"), None),
    )
    out_specs = P(("groups", "rows"), None)
    return jax.shard_map(
        on_device, mesh=mesh, in_specs=in_specs, out_specs=out_specs, check_vma=False
    )
```

```python
import functools
import math

import jax
import jax.numpy as jnp
from jax import lax
from jax.experimental import pallas as pl
from jax.experimental.pallas import tpu as pltpu
from jax.sharding import PartitionSpec as P

TOPK = 8
BF16 = jnp.bfloat16
F32 = jnp.float32


gate_scale = 1.0 / 1024.0


def rms_scale(features, norm_gain):
    mean_square = jnp.mean(features * features, axis=-1, keepdims=True)
    return features * lax.rsqrt(mean_square + 1e-06) * norm_gain


def ring_plan(devices):
    chips = devices // 2
    order = list(range(0, chips, 2)) + list(range(chips - 1, 0, -2))
    swap = [(device, device ^ 1) for device in range(devices)]

    def toward(step):
        pairs = []
        for place in range(chips):
            for core in range(2):
                target = order[(place + step * (1 - 2 * core)) % chips]
                pairs.append((2 * order[place] + core, 2 * target + core))
        return pairs

    return order, toward, swap


VMEM = pl.BlockSpec(memory_space=pltpu.VMEM)
SMEM = pl.BlockSpec(memory_space=pltpu.SMEM)


def ring_view(chips):
    me = lax.axis_index("rows")
    chip, core = lax.div(me, 2), lax.rem(me, 2)
    half = lax.div(chip, 2)
    place = jnp.where(lax.rem(chip, 2) == 0, half, chips - 1 - half)

    def chip_at(offset):
        there = lax.rem(place + (1 - 2 * core) * offset + chips, chips)
        return jnp.where(there < chips // 2, 2 * there, 2 * (chips - 1 - there) + 1)

    return chip, core, chip_at


def attend_kernel(
    chips,
    hops,
    chip_experts,
    lengths_ref,
    q_ref,
    k_ref,
    v_ref,
    ids_ref,
    numer_ref,
    *refs,
):
    far_ref, give_ref, own_ref = refs[:3]
    mine_refs, (q_rows, out_rows, tokens) = refs[3 : hops + 2], refs[hops + 2 :]
    step, steps = pl.program_id(0), pl.num_programs(0)
    block, kv_count, cache_len, head_size = k_ref.shape
    rows, feats = q_ref.shape
    heads = feats // head_size
    group = heads // kv_count

    @pl.when(step == 0)
    def _():
        for head in range(heads):
            q_rows[pl.ds(head, rows, stride=heads), :] = q_ref[
                :, head * head_size : (head + 1) * head_size
            ].astype(F32)

    head_of = lax.broadcasted_iota(jnp.int32, (block, heads, cache_len), 1) // group
    slot = lax.broadcasted_iota(jnp.int32, (heads, cache_len), 1)
    first = pl.multiple_of(step * block * heads, block * heads)
    asked = q_rows[pl.ds(first, block * heads), :].astype(BF16)
    scores = [
        lax.dot_general(
            asked[i * heads : (i + 1) * heads],
            k_ref[i].reshape(kv_count * cache_len, head_size),
            (((1,), (1,)), ((), ())),
            preferred_element_type=F32,
        )
        for i in range(block)
    ]
    scores = jnp.stack(scores)
    live = jnp.stack([slot < lengths_ref[step * block + i] for i in range(block)])
    picked = scores[:, :, :cache_len]
    for kv in range(1, kv_count):
        picked = jnp.where(
            head_of == kv, scores[:, :, kv * cache_len : (kv + 1) * cache_len], picked
        )
    picked = jnp.where(live, picked * (1.0 / math.sqrt(head_size)), -1e30)
    weights = jnp.exp(picked - jnp.max(picked, axis=2, keepdims=True))
    shares = weights / jnp.sum(weights, axis=2, keepdims=True)
    spread = jnp.concatenate(
        [jnp.where(head_of == kv, shares, 0.0) for kv in range(kv_count)], axis=2
    ).astype(BF16)
    for i in range(block):
        values = v_ref[i].reshape(kv_count * cache_len, head_size)
        out_rows[pl.ds(first + i * heads, heads), :] = jnp.dot(
            spread[i], values, preferred_element_type=F32
        )

    @pl.when(step == steps - 1)
    def _():
        chip_heads = heads // chips
        chip_feats = chip_heads * head_size
        for head in range(heads):
            start = (head % chip_heads) * head_size
            tokens[head // chip_heads, :, start : start + head_size] = out_rows[
                pl.ds(head, rows, stride=heads), :
            ].astype(BF16)
        extra = tokens.shape[2] - chip_feats
        choices = ids_ref.shape[0]
        total = chips * chip_experts
        expert = lax.broadcasted_iota(jnp.int32, (total, rows), 0)
        found = jnp.zeros((total, rows), jnp.int32)
        for j in range(choices):
            found += jnp.where(ids_ref[j : j + 1, :] == expert, numer_ref[j : j + 1, :], 0)
        digits = jnp.concatenate([found >> 4, found & 15], axis=0).astype(F32).astype(BF16)
        source = lax.broadcasted_iota(jnp.int32, (2 * total, extra), 0)
        lane = lax.broadcasted_iota(jnp.int32, (2 * total, extra), 1)
        for there in range(chips):
            base = there * chip_experts
            wanted = jnp.where(lane < chip_experts, base + lane, total + base + lane - chip_experts)
            pick = (source == wanted) & (lane < 2 * chip_experts)
            tokens[there, :, chip_feats:] = lax.dot_general(
                digits,
                jnp.where(pick, 1.0, 0.0).astype(BF16),
                (((0,), (0,)), ((), ())),
                preferred_element_type=F32,
            ).astype(BF16)
        chip, _, chip_at = ring_view(chips)
        far_ref[...] = tokens[chip_at(-hops)]
        own_ref[...] = tokens[chip]
        for offset in range(1, hops):
            mine_refs[offset - 1][...] = tokens[chip_at(-offset)]
            give_ref[offset - 1] = tokens[chip_at(offset)]


def attend(devices, chip_experts, queries, cache_keys, cache_values, lengths, ids, numer):
    chips, hops = devices // 2, devices // 4
    rows, feats = queries.shape
    kv_count, cache_len, head_size = cache_keys.shape[1:]
    heads = feats // head_size
    extra = -(-2 * chip_experts // 128) * 128
    wide = feats // chips + extra
    block = 16
    cache = pl.BlockSpec((block, kv_count, cache_len, head_size), lambda t: (t, 0, 0, 0))
    one = jax.ShapeDtypeStruct((rows, wide), BF16)
    several = jax.ShapeDtypeStruct((hops - 1, rows, wide), BF16)
    return pl.pallas_call(
        functools.partial(attend_kernel, chips, hops, chip_experts),
        out_shape=(one, several) + (one,) * hops,
        grid=(rows // block,),
        in_specs=[SMEM, VMEM, cache, cache, VMEM, VMEM],
        out_specs=(VMEM,) * (hops + 2),
        scratch_shapes=[
            pltpu.VMEM((rows * heads, head_size), F32),
            pltpu.VMEM((rows * heads, head_size), F32),
            pltpu.VMEM((chips, rows, wide), BF16),
        ],
        compiler_params=pltpu.CompilerParams(vmem_limit_bytes=54 * 1024 * 1024),
        cost_estimate=pl.CostEstimate(
            flops=4 * rows * heads * cache_len * head_size,
            bytes_accessed=4 * rows * kv_count * cache_len * head_size,
            transcendentals=rows * heads * cache_len,
        ),
    )(lengths, queries, cache_keys, cache_values, ids.T, numer.T)


def project_kernel(pieces, *refs):
    piece_refs, own_ref, other_ref = refs[:pieces], refs[pieces], refs[pieces + 1]
    out_refs, x_ref = refs[pieces + 2 : -1], refs[-1]
    feats, width = own_ref.shape
    start = 0
    for piece in piece_refs:
        x_ref[start : start + piece.shape[0], :] = piece[:, : 2 * feats]
        start += piece.shape[0]

    def both(first, second):
        tile = 512
        for column in range(0, width, tile):
            done = jnp.dot(
                x_ref[:, :feats], first[:, column : column + tile], preferred_element_type=F32
            ) + jnp.dot(
                x_ref[:, feats:], second[:, column : column + tile], preferred_element_type=F32
            )
            start = 0
            for out in out_refs:
                out[:, column : column + tile] = done[start : start + out.shape[0]].astype(
                    out.dtype
                )
                start += out.shape[0]

    core = lax.rem(lax.axis_index("rows"), 2)

    @pl.when(core == 0)
    def _():
        both(own_ref, other_ref)

    @pl.when(core == 1)
    def _():
        both(other_ref, own_ref)


def project(pieces, kinds, own, other):
    feats, width = own.shape
    rows = sum(piece.shape[0] for piece in pieces)
    return pl.pallas_call(
        functools.partial(project_kernel, len(pieces)),
        out_shape=tuple(
            jax.ShapeDtypeStruct((rows // len(kinds), width), kind) for kind in kinds
        ),
        in_specs=[VMEM] * (len(pieces) + 2),
        out_specs=(VMEM,) * len(kinds),
        scratch_shapes=[pltpu.VMEM((rows, 2 * feats), BF16)],
        compiler_params=pltpu.CompilerParams(vmem_limit_bytes=32 * 1024 * 1024),
        cost_estimate=pl.CostEstimate(
            flops=4 * rows * feats * width, bytes_accessed=4 * feats * width, transcendentals=0
        ),
    )(*pieces, own, other)


def expert_kernel(pieces, blocks, local, local_experts, *refs):
    piece_refs, digit_refs, refs = refs[:pieces], refs[pieces : pieces + blocks], refs[pieces + blocks :]
    weight_refs, refs = refs[:6], refs[6:]
    out_refs, (x_ref, inner_ref, gates_ref) = refs[:pieces], refs[pieces:]
    size = piece_refs[0].shape[0]
    for index, piece in enumerate(piece_refs):
        x_ref[index * size : (index + 1) * size, :] = piece[...]
    core = lax.rem(lax.axis_index("rows"), 2)
    chip_experts = 2 * local_experts
    start = 0
    for digits in digit_refs:
        feats = digits.shape[1] - 128 * (-(-2 * chip_experts // 128))
        taken = digits[:, feats:].astype(F32)

        def gate(k):
            high, low = taken[:, k : k + 1], taken[:, chip_experts + k : chip_experts + k + 1]
            return (high * 16.0 + low) * gate_scale

        first, second = gate(local), gate(local_experts + local)
        stop = start + digits.shape[0]
        gates_ref[0, start:stop, :] = jnp.where(core == 0, first, second)
        gates_ref[1, start:stop, :] = jnp.where(core == 0, second, first)
        start = stop
    gates = (gates_ref[0], gates_ref[1])
    hidden_units, width = weight_refs[2].shape[1:]
    tile = 256
    for which in range(2):
        w_gate, w_up = weight_refs[3 * which], weight_refs[3 * which + 1]
        for start in range(0, hidden_units, tile):
            gate_proj = jnp.dot(
                x_ref[...], w_gate[local, :, start : start + tile], preferred_element_type=F32
            )
            raised = jnp.dot(
                x_ref[...], w_up[local, :, start : start + tile], preferred_element_type=F32
            )
            inner = jax.nn.silu(gate_proj) * raised * gates[which]
            place = which * hidden_units + start
            inner_ref[:, place : place + tile] = inner.astype(BF16)
    tile = 512
    for start in range(0, width, tile):
        done = jnp.dot(
            inner_ref[:, :hidden_units],
            weight_refs[2][local, :, start : start + tile],
            preferred_element_type=F32,
        ) + jnp.dot(
            inner_ref[:, hidden_units:],
            weight_refs[5][local, :, start : start + tile],
            preferred_element_type=F32,
        )
        for index, out in enumerate(out_refs):
            out[:, start : start + tile] = done[index * size : (index + 1) * size].astype(
                out.dtype
            )


def experts(pieces, kinds, digits, own, other, local):
    local_experts, width, hidden_units = own[0].shape
    rows = sum(piece.shape[0] for piece in pieces)
    return pl.pallas_call(
        functools.partial(expert_kernel, len(pieces), len(digits), local, local_experts),
        out_shape=tuple(
            jax.ShapeDtypeStruct((piece.shape[0], width), kind)
            for piece, kind in zip(pieces, kinds)
        ),
        in_specs=[VMEM] * (len(pieces) + len(digits) + 6),
        out_specs=(VMEM,) * len(pieces),
        scratch_shapes=[
            pltpu.VMEM((rows, width), BF16),
            pltpu.VMEM((rows, 2 * hidden_units), BF16),
            pltpu.VMEM((2, rows, 1), F32),
        ],
        compiler_params=pltpu.CompilerParams(vmem_limit_bytes=16 * 1024 * 1024),
        cost_estimate=pl.CostEstimate(
            flops=12 * rows * hidden_units * width,
            bytes_accessed=rows * width,
            transcendentals=2 * rows * hidden_units,
        ),
    )(*pieces, *digits, *own, *other)


def on_device(
    queries,
    cache_keys,
    cache_values,
    lengths,
    hidden,
    out_weight,
    norm_gain,
    w_gate,
    w_up,
    w_down,
    expert_ids,
    gate_numer,
):
    devices = lax.axis_size("rows")
    hops = devices // 4
    local_experts = w_gate.shape[0]
    order, toward, swap = ring_plan(devices)

    def pass_on(array, step):
        return lax.ppermute(array, "rows", toward(step))

    def swapped(array):
        return lax.ppermute(array, "rows", swap)

    weight_other = swapped(out_weight)
    own_experts = (w_gate, w_up, w_down)

    far, give, here, *mine = attend(
        devices,
        2 * local_experts,
        queries,
        cache_keys,
        cache_values,
        lengths,
        expert_ids,
        gate_numer,
    )
    got = swapped(give)

    def send(offset, mine, got):
        return pass_on(jnp.concatenate([mine, got], axis=0), -offset)

    kinds = [BF16, F32, BF16] + [F32] * (2 * hops - 3)
    weights = (out_weight, weight_other)
    arrived = {0: here, hops: pass_on(far, -hops)}
    arrived[hops - 1] = send(hops - 1, mine[hops - 2], got[hops - 2])
    partial = project([arrived[hops], arrived[hops - 1]], kinds[:3], *weights)
    first = pass_on(partial[0], 1)
    first, mine, got, own_experts = lax.optimization_barrier((first, mine, got, own_experts))
    for offset in range(hops - 2, 0, -1):
        arrived[offset] = send(offset, mine[offset - 1], got[offset - 1])
    partial += project(
        [arrived[offset] for offset in range(hops - 2, -1, -1)], kinds[3:], *weights
    )
    other_experts = tuple(swapped(w) for w in own_experts)

    def ring_sums(partial, first):
        own, other = first, partial[2]
        for offset in range(hops - 1, 0, -1):
            spot = 1 + 2 * (hops - 1 - offset)
            if offset < hops - 1:
                other = (pass_on(other, 1).astype(F32) + partial[spot + 1]).astype(BF16)
            if offset < hops - 1:
                own = pass_on(own, 1)
            own = (own.astype(F32) + partial[spot]).astype(BF16)
        other = swapped(pass_on(other, 1)).astype(F32)
        return pass_on(own, 1).astype(F32) + partial[-1] + other

    residual = (hidden.astype(F32) + ring_sums(partial, first)).astype(BF16)
    normed = rms_scale(residual.astype(F32), norm_gain).astype(BF16)

    def serve(pieces, kinds, digits):
        total = None
        for local in range(local_experts):
            plain = kinds if local_experts == 1 else [F32] * len(kinds)
            served = experts(pieces, plain, digits, own_experts, other_experts, local)
            total = served if local == 0 else [a + b for a, b in zip(total, served)]
        return [part.astype(kind) for part, kind in zip(total, kinds)]

    own, other = normed, swapped(normed)
    pieces = [own]
    for offset in range(1, hops):
        own, other = pass_on(own, -1), pass_on(other, -1)
        pieces = [own, other] + pieces
    pieces = [pass_on(own, -1)] + pieces
    digits = [arrived[offset] for offset in range(hops, -1, -1)]
    total = serve(pieces[:3], kinds[:3], digits[:2]) + serve(pieces[3:], kinds[3:], digits[2:])
    return (residual.astype(F32) + ring_sums(total, pass_on(total[0], 1))).astype(BF16)


def solution(mesh):
    in_specs = (
        P(("groups", "rows"), None),
        P(("groups", "rows"), None, None, None),
        P(("groups", "rows"), None, None, None),
        P(("groups", "rows")),
        P(("groups", "rows"), None),
        P("rows", None),
        P(),
        P("rows", None, None),
        P("rows", None, None),
        P("rows", None, None),
        P(("groups", "rows"), None),
        P(("groups", "rows"), None),
    )
    out_specs = P(("groups", "rows"), None)
    return jax.shard_map(
        on_device, mesh=mesh, in_specs=in_specs, out_specs=out_specs, check_vma=False
    )
```

```python
import functools
import math

import jax
import jax.numpy as jnp
from jax import lax
from jax.experimental import pallas as pl
from jax.experimental.pallas import tpu as pltpu
from jax.sharding import PartitionSpec as P

TOPK = 8
BF16 = jnp.bfloat16
F32 = jnp.float32


gate_scale = 1.0 / 1024.0


def rms_scale(features, norm_gain):
    mean_square = jnp.mean(features * features, axis=-1, keepdims=True)
    return features * lax.rsqrt(mean_square + 1e-06) * norm_gain


def ring_plan(devices):
    chips = devices // 2
    order = list(range(0, chips, 2)) + list(range(chips - 1, 0, -2))
    swap = [(device, device ^ 1) for device in range(devices)]

    def toward(step):
        pairs = []
        for place in range(chips):
            for core in range(2):
                target = order[(place + step * (1 - 2 * core)) % chips]
                pairs.append((2 * order[place] + core, 2 * target + core))
        return pairs

    return order, toward, swap


VMEM = pl.BlockSpec(memory_space=pltpu.VMEM)
SMEM = pl.BlockSpec(memory_space=pltpu.SMEM)


def ring_view(chips):
    me = lax.axis_index("rows")
    chip, core = lax.div(me, 2), lax.rem(me, 2)
    half = lax.div(chip, 2)
    place = jnp.where(lax.rem(chip, 2) == 0, half, chips - 1 - half)

    def chip_at(offset):
        there = lax.rem(place + (1 - 2 * core) * offset + chips, chips)
        return jnp.where(there < chips // 2, 2 * there, 2 * (chips - 1 - there) + 1)

    return chip, core, chip_at


def attend_kernel(
    chips,
    hops,
    chip_experts,
    lengths_ref,
    q_ref,
    k_ref,
    v_ref,
    ids_ref,
    numer_ref,
    *refs,
):
    far_ref, give_ref, own_ref = refs[:3]
    mine_refs, (q_rows, out_rows, tokens) = refs[3 : hops + 2], refs[hops + 2 :]
    step, steps = pl.program_id(0), pl.num_programs(0)
    block, kv_count, cache_len, head_size = k_ref.shape
    rows, feats = q_ref.shape
    heads = feats // head_size
    group = heads // kv_count

    @pl.when(step == 0)
    def _():
        for head in range(heads):
            q_rows[pl.ds(head, rows, stride=heads), :] = q_ref[
                :, head * head_size : (head + 1) * head_size
            ].astype(F32)

    head_of = lax.broadcasted_iota(jnp.int32, (block, heads, cache_len), 1) // group
    slot = lax.broadcasted_iota(jnp.int32, (heads, cache_len), 1)
    first = pl.multiple_of(step * block * heads, block * heads)
    asked = q_rows[pl.ds(first, block * heads), :].astype(BF16)
    scores = [
        lax.dot_general(
            asked[i * heads : (i + 1) * heads],
            k_ref[i].reshape(kv_count * cache_len, head_size),
            (((1,), (1,)), ((), ())),
            preferred_element_type=F32,
        )
        for i in range(block)
    ]
    scores = jnp.stack(scores)
    live = jnp.stack([slot < lengths_ref[step * block + i] for i in range(block)])
    picked = scores[:, :, :cache_len]
    for kv in range(1, kv_count):
        picked = jnp.where(
            head_of == kv, scores[:, :, kv * cache_len : (kv + 1) * cache_len], picked
        )
    picked = jnp.where(live, picked * (1.0 / math.sqrt(head_size)), -1e30)
    weights = jnp.exp(picked - jnp.max(picked, axis=2, keepdims=True))
    shares = weights / jnp.sum(weights, axis=2, keepdims=True)
    spread = jnp.concatenate(
        [jnp.where(head_of == kv, shares, 0.0) for kv in range(kv_count)], axis=2
    ).astype(BF16)
    for i in range(block):
        values = v_ref[i].reshape(kv_count * cache_len, head_size)
        out_rows[pl.ds(first + i * heads, heads), :] = jnp.dot(
            spread[i], values, preferred_element_type=F32
        )

    @pl.when(step == steps - 1)
    def _():
        chip_heads = heads // chips
        chip_feats = chip_heads * head_size
        for head in range(heads):
            start = (head % chip_heads) * head_size
            tokens[head // chip_heads, :, start : start + head_size] = out_rows[
                pl.ds(head, rows, stride=heads), :
            ].astype(BF16)
        extra = tokens.shape[2] - chip_feats
        choices = ids_ref.shape[0]
        total = chips * chip_experts
        expert = lax.broadcasted_iota(jnp.int32, (total, rows), 0)
        found = jnp.zeros((total, rows), jnp.int32)
        for j in range(choices):
            found += jnp.where(ids_ref[j : j + 1, :] == expert, numer_ref[j : j + 1, :], 0)
        digits = jnp.concatenate([found >> 4, found & 15], axis=0).astype(F32).astype(BF16)
        source = lax.broadcasted_iota(jnp.int32, (2 * total, extra), 0)
        lane = lax.broadcasted_iota(jnp.int32, (2 * total, extra), 1)
        for there in range(chips):
            base = there * chip_experts
            wanted = jnp.where(lane < chip_experts, base + lane, total + base + lane - chip_experts)
            pick = (source == wanted) & (lane < 2 * chip_experts)
            tokens[there, :, chip_feats:] = lax.dot_general(
                digits,
                jnp.where(pick, 1.0, 0.0).astype(BF16),
                (((0,), (0,)), ((), ())),
                preferred_element_type=F32,
            ).astype(BF16)
        chip, _, chip_at = ring_view(chips)
        far_ref[...] = tokens[chip_at(-hops)]
        own_ref[...] = tokens[chip]
        for offset in range(1, hops):
            mine_refs[offset - 1][...] = tokens[chip_at(-offset)]
            give_ref[offset - 1] = tokens[chip_at(offset)]


def attend(devices, chip_experts, queries, cache_keys, cache_values, lengths, ids, numer):
    chips, hops = devices // 2, devices // 4
    rows, feats = queries.shape
    kv_count, cache_len, head_size = cache_keys.shape[1:]
    heads = feats // head_size
    extra = -(-2 * chip_experts // 128) * 128
    wide = feats // chips + extra
    block = 32
    cache = pl.BlockSpec((block, kv_count, cache_len, head_size), lambda t: (t, 0, 0, 0))
    one = jax.ShapeDtypeStruct((rows, wide), BF16)
    several = jax.ShapeDtypeStruct((hops - 1, rows, wide), BF16)
    return pl.pallas_call(
        functools.partial(attend_kernel, chips, hops, chip_experts),
        out_shape=(one, several) + (one,) * hops,
        grid=(rows // block,),
        in_specs=[SMEM, VMEM, cache, cache, VMEM, VMEM],
        out_specs=(VMEM,) * (hops + 2),
        scratch_shapes=[
            pltpu.VMEM((rows * heads, head_size), F32),
            pltpu.VMEM((rows * heads, head_size), F32),
            pltpu.VMEM((chips, rows, wide), BF16),
        ],
        compiler_params=pltpu.CompilerParams(vmem_limit_bytes=54 * 1024 * 1024),
        cost_estimate=pl.CostEstimate(
            flops=4 * rows * heads * cache_len * head_size,
            bytes_accessed=4 * rows * kv_count * cache_len * head_size,
            transcendentals=rows * heads * cache_len,
        ),
    )(lengths, queries, cache_keys, cache_values, ids.T, numer.T)


def project_kernel(pieces, *refs):
    piece_refs, own_ref, other_ref = refs[:pieces], refs[pieces], refs[pieces + 1]
    out_refs, x_ref = refs[pieces + 2 : -1], refs[-1]
    feats, width = own_ref.shape
    start = 0
    for piece in piece_refs:
        x_ref[start : start + piece.shape[0], :] = piece[:, : 2 * feats]
        start += piece.shape[0]

    def both(first, second):
        tile = 512
        for column in range(0, width, tile):
            done = jnp.dot(
                x_ref[:, :feats], first[:, column : column + tile], preferred_element_type=F32
            ) + jnp.dot(
                x_ref[:, feats:], second[:, column : column + tile], preferred_element_type=F32
            )
            start = 0
            for out in out_refs:
                out[:, column : column + tile] = done[start : start + out.shape[0]].astype(
                    out.dtype
                )
                start += out.shape[0]

    core = lax.rem(lax.axis_index("rows"), 2)

    @pl.when(core == 0)
    def _():
        both(own_ref, other_ref)

    @pl.when(core == 1)
    def _():
        both(other_ref, own_ref)


def project(pieces, kinds, own, other):
    feats, width = own.shape
    rows = sum(piece.shape[0] for piece in pieces)
    return pl.pallas_call(
        functools.partial(project_kernel, len(pieces)),
        out_shape=tuple(
            jax.ShapeDtypeStruct((rows // len(kinds), width), kind) for kind in kinds
        ),
        in_specs=[VMEM] * (len(pieces) + 2),
        out_specs=(VMEM,) * len(kinds),
        scratch_shapes=[pltpu.VMEM((rows, 2 * feats), BF16)],
        compiler_params=pltpu.CompilerParams(vmem_limit_bytes=32 * 1024 * 1024),
        cost_estimate=pl.CostEstimate(
            flops=4 * rows * feats * width, bytes_accessed=4 * feats * width, transcendentals=0
        ),
    )(*pieces, own, other)


def expert_kernel(pieces, blocks, local, local_experts, *refs):
    piece_refs, digit_refs, refs = refs[:pieces], refs[pieces : pieces + blocks], refs[pieces + blocks :]
    weight_refs, refs = refs[:6], refs[6:]
    out_refs, (x_ref, inner_ref, gates_ref) = refs[:pieces], refs[pieces:]
    size = piece_refs[0].shape[0]
    for index, piece in enumerate(piece_refs):
        x_ref[index * size : (index + 1) * size, :] = piece[...]
    core = lax.rem(lax.axis_index("rows"), 2)
    chip_experts = 2 * local_experts
    start = 0
    for digits in digit_refs:
        feats = digits.shape[1] - 128 * (-(-2 * chip_experts // 128))
        taken = digits[:, feats:].astype(F32)

        def gate(k):
            high, low = taken[:, k : k + 1], taken[:, chip_experts + k : chip_experts + k + 1]
            return (high * 16.0 + low) * gate_scale

        first, second = gate(local), gate(local_experts + local)
        stop = start + digits.shape[0]
        gates_ref[0, start:stop, :] = jnp.where(core == 0, first, second)
        gates_ref[1, start:stop, :] = jnp.where(core == 0, second, first)
        start = stop
    gates = (gates_ref[0], gates_ref[1])
    hidden_units, width = weight_refs[2].shape[1:]
    tile = 256
    for which in range(2):
        w_gate, w_up = weight_refs[3 * which], weight_refs[3 * which + 1]
        for start in range(0, hidden_units, tile):
            gate_proj = jnp.dot(
                x_ref[...], w_gate[local, :, start : start + tile], preferred_element_type=F32
            )
            raised = jnp.dot(
                x_ref[...], w_up[local, :, start : start + tile], preferred_element_type=F32
            )
            inner = jax.nn.silu(gate_proj) * raised * gates[which]
            place = which * hidden_units + start
            inner_ref[:, place : place + tile] = inner.astype(BF16)
    tile = 512
    for start in range(0, width, tile):
        done = jnp.dot(
            inner_ref[:, :hidden_units],
            weight_refs[2][local, :, start : start + tile],
            preferred_element_type=F32,
        ) + jnp.dot(
            inner_ref[:, hidden_units:],
            weight_refs[5][local, :, start : start + tile],
            preferred_element_type=F32,
        )
        for index, out in enumerate(out_refs):
            out[:, start : start + tile] = done[index * size : (index + 1) * size].astype(
                out.dtype
            )


def experts(pieces, kinds, digits, own, other, local):
    local_experts, width, hidden_units = own[0].shape
    rows = sum(piece.shape[0] for piece in pieces)
    return pl.pallas_call(
        functools.partial(expert_kernel, len(pieces), len(digits), local, local_experts),
        out_shape=tuple(
            jax.ShapeDtypeStruct((piece.shape[0], width), kind)
            for piece, kind in zip(pieces, kinds)
        ),
        in_specs=[VMEM] * (len(pieces) + len(digits) + 6),
        out_specs=(VMEM,) * len(pieces),
        scratch_shapes=[
            pltpu.VMEM((rows, width), BF16),
            pltpu.VMEM((rows, 2 * hidden_units), BF16),
            pltpu.VMEM((2, rows, 1), F32),
        ],
        compiler_params=pltpu.CompilerParams(vmem_limit_bytes=16 * 1024 * 1024),
        cost_estimate=pl.CostEstimate(
            flops=12 * rows * hidden_units * width,
            bytes_accessed=rows * width,
            transcendentals=2 * rows * hidden_units,
        ),
    )(*pieces, *digits, *own, *other)


def on_device(
    queries,
    cache_keys,
    cache_values,
    lengths,
    hidden,
    out_weight,
    norm_gain,
    w_gate,
    w_up,
    w_down,
    expert_ids,
    gate_numer,
):
    devices = lax.axis_size("rows")
    hops = devices // 4
    local_experts = w_gate.shape[0]
    order, toward, swap = ring_plan(devices)

    def pass_on(array, step):
        return lax.ppermute(array, "rows", toward(step))

    def swapped(array):
        return lax.ppermute(array, "rows", swap)

    weight_other = swapped(out_weight)
    own_experts = (w_gate, w_up, w_down)

    far, give, here, *mine = attend(
        devices,
        2 * local_experts,
        queries,
        cache_keys,
        cache_values,
        lengths,
        expert_ids,
        gate_numer,
    )
    got = swapped(give)

    def send(offset, mine, got):
        return pass_on(jnp.concatenate([mine, got], axis=0), -offset)

    kinds = [BF16, BF16, BF16] + [F32] * (2 * hops - 3)
    weights = (out_weight, weight_other)
    arrived = {0: here, hops: pass_on(far, -hops)}
    arrived[hops - 1] = send(hops - 1, mine[hops - 2], got[hops - 2])
    partial = project([arrived[hops], arrived[hops - 1]], kinds[:3], *weights)
    first = pass_on(partial[0], 2)
    first, own_experts = lax.optimization_barrier((first, own_experts))
    for offset in range(hops - 2, 0, -1):
        arrived[offset] = send(offset, mine[offset - 1], got[offset - 1])
    partial += project(
        [arrived[offset] for offset in range(hops - 2, -1, -1)], kinds[3:], *weights
    )
    other_experts = tuple(swapped(w) for w in own_experts)

    def ring_sums(partial, far):
        own, other = partial[1].astype(BF16), partial[2]
        for offset in range(hops - 2, 0, -1):
            spot = 1 + 2 * (hops - 1 - offset)
            own = pass_on(own, 1).astype(F32) + partial[spot]
            if offset == hops - 2:
                own = own + far.astype(F32)
            own = own.astype(BF16)
            other = (pass_on(other, 1).astype(F32) + partial[spot + 1]).astype(BF16)
        other = swapped(pass_on(other, 1)).astype(F32)
        return pass_on(own, 1).astype(F32) + partial[-1] + other

    residual = (hidden.astype(F32) + ring_sums(partial, first)).astype(BF16)
    normed = rms_scale(residual.astype(F32), norm_gain).astype(BF16)

    def serve(pieces, kinds, digits):
        total = None
        for local in range(local_experts):
            plain = kinds if local_experts == 1 else [F32] * len(kinds)
            served = experts(pieces, plain, digits, own_experts, other_experts, local)
            total = served if local == 0 else [a + b for a, b in zip(total, served)]
        return [part.astype(kind) for part, kind in zip(total, kinds)]

    own, other = normed, swapped(normed)
    pieces = [own]
    for offset in range(1, hops):
        own, other = pass_on(own, -1), pass_on(other, -1)
        pieces = [own, other] + pieces
    pieces = [pass_on(own, -1)] + pieces
    digits = [arrived[offset] for offset in range(hops, -1, -1)]
    total = serve(pieces[:3], kinds[:3], digits[:2]) + serve(pieces[3:], kinds[3:], digits[2:])
    return (residual.astype(F32) + ring_sums(total, pass_on(total[0], 2))).astype(BF16)


def solution(mesh):
    in_specs = (
        P(("groups", "rows"), None),
        P(("groups", "rows"), None, None, None),
        P(("groups", "rows"), None, None, None),
        P(("groups", "rows")),
        P(("groups", "rows"), None),
        P("rows", None),
        P(),
        P("rows", None, None),
        P("rows", None, None),
        P("rows", None, None),
        P(("groups", "rows"), None),
        P(("groups", "rows"), None),
    )
    out_specs = P(("groups", "rows"), None)
    return jax.shard_map(
        on_device, mesh=mesh, in_specs=in_specs, out_specs=out_specs, check_vma=False
    )
```

```python
import functools
import math

import jax
import jax.numpy as jnp
from jax import lax
from jax.experimental import pallas as pl
from jax.experimental.pallas import tpu as pltpu
from jax.sharding import PartitionSpec as P

TOPK = 8
BF16 = jnp.bfloat16
F32 = jnp.float32


gate_scale = 1.0 / 1024.0


def rms_scale(features, norm_gain):
    mean_square = jnp.mean(features * features, axis=-1, keepdims=True)
    return features * lax.rsqrt(mean_square + 1e-06) * norm_gain


def ring_plan(devices):
    chips = devices // 2
    order = list(range(0, chips, 2)) + list(range(chips - 1, 0, -2))
    swap = [(device, device ^ 1) for device in range(devices)]

    def toward(step):
        pairs = []
        for place in range(chips):
            for core in range(2):
                target = order[(place + step * (1 - 2 * core)) % chips]
                pairs.append((2 * order[place] + core, 2 * target + core))
        return pairs

    return order, toward, swap


VMEM = pl.BlockSpec(memory_space=pltpu.VMEM)
SMEM = pl.BlockSpec(memory_space=pltpu.SMEM)


def ring_view(chips):
    me = lax.axis_index("rows")
    chip, core = lax.div(me, 2), lax.rem(me, 2)
    half = lax.div(chip, 2)
    place = jnp.where(lax.rem(chip, 2) == 0, half, chips - 1 - half)

    def chip_at(offset):
        there = lax.rem(place + (1 - 2 * core) * offset + chips, chips)
        return jnp.where(there < chips // 2, 2 * there, 2 * (chips - 1 - there) + 1)

    return chip, core, chip_at


def attend_kernel(
    chips,
    hops,
    chip_experts,
    lengths_ref,
    q_ref,
    k_ref,
    v_ref,
    ids_ref,
    numer_ref,
    *refs,
):
    far_ref, give_ref, own_ref = refs[:3]
    mine_refs, (q_rows, out_rows, tokens) = refs[3 : hops + 2], refs[hops + 2 :]
    step, steps = pl.program_id(0), pl.num_programs(0)
    block, kv_count, cache_len, head_size = k_ref.shape
    rows, feats = q_ref.shape
    heads = feats // head_size
    group = heads // kv_count

    @pl.when(step == 0)
    def _():
        for head in range(heads):
            q_rows[pl.ds(head, rows, stride=heads), :] = q_ref[
                :, head * head_size : (head + 1) * head_size
            ].astype(F32)

    head_of = lax.broadcasted_iota(jnp.int32, (block, heads, cache_len), 1) // group
    slot = lax.broadcasted_iota(jnp.int32, (heads, cache_len), 1)
    first = pl.multiple_of(step * block * heads, block * heads)
    asked = q_rows[pl.ds(first, block * heads), :].astype(BF16)
    scores = [
        lax.dot_general(
            asked[i * heads : (i + 1) * heads],
            k_ref[i].reshape(kv_count * cache_len, head_size),
            (((1,), (1,)), ((), ())),
            preferred_element_type=F32,
        )
        for i in range(block)
    ]
    scores = jnp.stack(scores)
    live = jnp.stack([slot < lengths_ref[step * block + i] for i in range(block)])
    picked = scores[:, :, :cache_len]
    for kv in range(1, kv_count):
        picked = jnp.where(
            head_of == kv, scores[:, :, kv * cache_len : (kv + 1) * cache_len], picked
        )
    picked = jnp.where(live, picked * (1.0 / math.sqrt(head_size)), -1e30)
    weights = jnp.exp(picked - jnp.max(picked, axis=2, keepdims=True))
    shares = weights / jnp.sum(weights, axis=2, keepdims=True)
    spread = jnp.concatenate(
        [jnp.where(head_of == kv, shares, 0.0) for kv in range(kv_count)], axis=2
    ).astype(BF16)
    for i in range(block):
        values = v_ref[i].reshape(kv_count * cache_len, head_size)
        out_rows[pl.ds(first + i * heads, heads), :] = jnp.dot(
            spread[i], values, preferred_element_type=F32
        )

    @pl.when(step == steps - 1)
    def _():
        chip_heads = heads // chips
        chip_feats = chip_heads * head_size
        for head in range(heads):
            start = (head % chip_heads) * head_size
            tokens[head // chip_heads, :, start : start + head_size] = out_rows[
                pl.ds(head, rows, stride=heads), :
            ].astype(BF16)
        extra = tokens.shape[2] - chip_feats
        choices = ids_ref.shape[0]
        total = chips * chip_experts
        expert = lax.broadcasted_iota(jnp.int32, (total, rows), 0)
        found = jnp.zeros((total, rows), jnp.int32)
        for j in range(choices):
            found += jnp.where(ids_ref[j : j + 1, :] == expert, numer_ref[j : j + 1, :], 0)
        digits = jnp.concatenate([found >> 4, found & 15], axis=0).astype(F32).astype(BF16)
        source = lax.broadcasted_iota(jnp.int32, (2 * total, extra), 0)
        lane = lax.broadcasted_iota(jnp.int32, (2 * total, extra), 1)
        for there in range(chips):
            base = there * chip_experts
            wanted = jnp.where(lane < chip_experts, base + lane, total + base + lane - chip_experts)
            pick = (source == wanted) & (lane < 2 * chip_experts)
            tokens[there, :, chip_feats:] = lax.dot_general(
                digits,
                jnp.where(pick, 1.0, 0.0).astype(BF16),
                (((0,), (0,)), ((), ())),
                preferred_element_type=F32,
            ).astype(BF16)
        chip, _, chip_at = ring_view(chips)
        far_ref[...] = tokens[chip_at(-hops)]
        own_ref[...] = tokens[chip]
        for offset in range(1, hops):
            mine_refs[offset - 1][...] = tokens[chip_at(-offset)]
            give_ref[offset - 1] = tokens[chip_at(offset)]


def attend(devices, chip_experts, queries, cache_keys, cache_values, lengths, ids, numer):
    chips, hops = devices // 2, devices // 4
    rows, feats = queries.shape
    kv_count, cache_len, head_size = cache_keys.shape[1:]
    heads = feats // head_size
    extra = -(-2 * chip_experts // 128) * 128
    wide = feats // chips + extra
    block = 32
    cache = pl.BlockSpec((block, kv_count, cache_len, head_size), lambda t: (t, 0, 0, 0))
    one = jax.ShapeDtypeStruct((rows, wide), BF16)
    several = jax.ShapeDtypeStruct((hops - 1, rows, wide), BF16)
    return pl.pallas_call(
        functools.partial(attend_kernel, chips, hops, chip_experts),
        out_shape=(one, several) + (one,) * hops,
        grid=(rows // block,),
        in_specs=[SMEM, VMEM, cache, cache, VMEM, VMEM],
        out_specs=(VMEM,) * (hops + 2),
        scratch_shapes=[
            pltpu.VMEM((rows * heads, head_size), F32),
            pltpu.VMEM((rows * heads, head_size), F32),
            pltpu.VMEM((chips, rows, wide), BF16),
        ],
        compiler_params=pltpu.CompilerParams(vmem_limit_bytes=54 * 1024 * 1024),
        cost_estimate=pl.CostEstimate(
            flops=4 * rows * heads * cache_len * head_size,
            bytes_accessed=4 * rows * kv_count * cache_len * head_size,
            transcendentals=rows * heads * cache_len,
        ),
    )(lengths, queries, cache_keys, cache_values, ids.T, numer.T)


def project_kernel(pieces, kept, *refs):
    piece_refs, own_ref, other_ref = refs[:pieces], refs[pieces], refs[pieces + 1]
    out_refs, x_ref = refs[pieces + 2 : -1], refs[-1]
    if kept:
        out_refs[-1][...] = own_ref[...]
        out_refs = out_refs[:-1]
    feats, width = own_ref.shape
    start = 0
    for piece in piece_refs:
        x_ref[start : start + piece.shape[0], :] = piece[:, : 2 * feats]
        start += piece.shape[0]

    def both(first, second):
        tile = 512
        for column in range(0, width, tile):
            done = jnp.dot(
                x_ref[:, :feats], first[:, column : column + tile], preferred_element_type=F32
            ) + jnp.dot(
                x_ref[:, feats:], second[:, column : column + tile], preferred_element_type=F32
            )
            start = 0
            for out in out_refs:
                out[:, column : column + tile] = done[start : start + out.shape[0]].astype(
                    out.dtype
                )
                start += out.shape[0]

    core = lax.rem(lax.axis_index("rows"), 2)

    @pl.when(core == 0)
    def _():
        both(own_ref, other_ref)

    @pl.when(core == 1)
    def _():
        both(other_ref, own_ref)


def project(pieces, kinds, own, other, kept=False):
    feats, width = own.shape
    rows = sum(piece.shape[0] for piece in pieces)
    return pl.pallas_call(
        functools.partial(project_kernel, len(pieces), kept),
        out_shape=tuple(
            jax.ShapeDtypeStruct((rows // len(kinds), width), kind) for kind in kinds
        )
        + (jax.ShapeDtypeStruct(own.shape, own.dtype),) * kept,
        in_specs=[VMEM] * (len(pieces) + 2),
        out_specs=(VMEM,) * (len(kinds) + kept),
        scratch_shapes=[pltpu.VMEM((rows, 2 * feats), BF16)],
        compiler_params=pltpu.CompilerParams(vmem_limit_bytes=32 * 1024 * 1024),
        cost_estimate=pl.CostEstimate(
            flops=4 * rows * feats * width, bytes_accessed=4 * feats * width, transcendentals=0
        ),
    )(*pieces, own, other)


def expert_kernel(pieces, blocks, local, local_experts, *refs):
    piece_refs, digit_refs, refs = refs[:pieces], refs[pieces : pieces + blocks], refs[pieces + blocks :]
    weight_refs, refs = refs[:6], refs[6:]
    out_refs, (x_ref, inner_ref, gates_ref) = refs[:pieces], refs[pieces:]
    size = piece_refs[0].shape[0]
    for index, piece in enumerate(piece_refs):
        x_ref[index * size : (index + 1) * size, :] = piece[...]
    core = lax.rem(lax.axis_index("rows"), 2)
    chip_experts = 2 * local_experts
    start = 0
    for digits in digit_refs:
        feats = digits.shape[1] - 128 * (-(-2 * chip_experts // 128))
        taken = digits[:, feats:].astype(F32)

        def gate(k):
            high, low = taken[:, k : k + 1], taken[:, chip_experts + k : chip_experts + k + 1]
            return (high * 16.0 + low) * gate_scale

        first, second = gate(local), gate(local_experts + local)
        stop = start + digits.shape[0]
        gates_ref[0, start:stop, :] = jnp.where(core == 0, first, second)
        gates_ref[1, start:stop, :] = jnp.where(core == 0, second, first)
        start = stop
    gates = (gates_ref[0], gates_ref[1])
    hidden_units, width = weight_refs[2].shape[1:]
    tile = 256
    for which in range(2):
        w_gate, w_up = weight_refs[3 * which], weight_refs[3 * which + 1]
        for start in range(0, hidden_units, tile):
            gate_proj = jnp.dot(
                x_ref[...], w_gate[local, :, start : start + tile], preferred_element_type=F32
            )
            raised = jnp.dot(
                x_ref[...], w_up[local, :, start : start + tile], preferred_element_type=F32
            )
            inner = jax.nn.silu(gate_proj) * raised * gates[which]
            place = which * hidden_units + start
            inner_ref[:, place : place + tile] = inner.astype(BF16)
    tile = 512
    for start in range(0, width, tile):
        done = jnp.dot(
            inner_ref[:, :hidden_units],
            weight_refs[2][local, :, start : start + tile],
            preferred_element_type=F32,
        ) + jnp.dot(
            inner_ref[:, hidden_units:],
            weight_refs[5][local, :, start : start + tile],
            preferred_element_type=F32,
        )
        for index, out in enumerate(out_refs):
            out[:, start : start + tile] = done[index * size : (index + 1) * size].astype(
                out.dtype
            )


def experts(pieces, kinds, digits, own, other, local):
    local_experts, width, hidden_units = own[0].shape
    rows = sum(piece.shape[0] for piece in pieces)
    return pl.pallas_call(
        functools.partial(expert_kernel, len(pieces), len(digits), local, local_experts),
        out_shape=tuple(
            jax.ShapeDtypeStruct((piece.shape[0], width), kind)
            for piece, kind in zip(pieces, kinds)
        ),
        in_specs=[VMEM] * (len(pieces) + len(digits) + 6),
        out_specs=(VMEM,) * len(pieces),
        scratch_shapes=[
            pltpu.VMEM((rows, width), BF16),
            pltpu.VMEM((rows, 2 * hidden_units), BF16),
            pltpu.VMEM((2, rows, 1), F32),
        ],
        compiler_params=pltpu.CompilerParams(vmem_limit_bytes=16 * 1024 * 1024),
        cost_estimate=pl.CostEstimate(
            flops=12 * rows * hidden_units * width,
            bytes_accessed=rows * width,
            transcendentals=2 * rows * hidden_units,
        ),
    )(*pieces, *digits, *own, *other)


def on_device(
    queries,
    cache_keys,
    cache_values,
    lengths,
    hidden,
    out_weight,
    norm_gain,
    w_gate,
    w_up,
    w_down,
    expert_ids,
    gate_numer,
):
    devices = lax.axis_size("rows")
    hops = devices // 4
    local_experts = w_gate.shape[0]
    order, toward, swap = ring_plan(devices)

    def pass_on(array, step):
        return lax.ppermute(array, "rows", toward(step))

    def swapped(array):
        return lax.ppermute(array, "rows", swap)

    weight_other = swapped(out_weight)
    own_experts = (w_gate, w_up, w_down)

    far, give, here, *mine = attend(
        devices,
        2 * local_experts,
        queries,
        cache_keys,
        cache_values,
        lengths,
        expert_ids,
        gate_numer,
    )
    got = swapped(give)

    def send(offset, mine, got):
        return pass_on(jnp.concatenate([mine, got], axis=0), -offset)

    kinds = [BF16, BF16, BF16] + [F32] * (2 * hops - 3)
    arrived = {0: here, hops: pass_on(far, -hops)}
    arrived[hops - 1] = send(hops - 1, mine[hops - 2], got[hops - 2])
    *partial, own_weight = project([arrived[hops]], kinds[:1], out_weight, weight_other, True)
    weights = (own_weight, weight_other)
    partial += project([arrived[hops - 1]], kinds[1:3], *weights)
    first = pass_on(partial[0], 2)
    first, own_experts = lax.optimization_barrier((first, own_experts))
    for offset in range(hops - 2, 0, -1):
        arrived[offset] = send(offset, mine[offset - 1], got[offset - 1])
    nearer = [arrived[offset] for offset in range(hops - 2, 0, -1)]
    partial += project(nearer, kinds[3:-1], *weights)
    partial += project([here], kinds[-1:], *weights)
    _, own_experts = lax.optimization_barrier((partial, own_experts))
    other_experts = tuple(swapped(w) for w in own_experts)

    def ring_sums(partial, far):
        own, other = partial[1].astype(BF16), partial[2]
        for offset in range(hops - 2, 0, -1):
            spot = 1 + 2 * (hops - 1 - offset)
            own = pass_on(own, 1).astype(F32) + partial[spot]
            if offset == hops - 2:
                own = own + far.astype(F32)
            own = own.astype(BF16)
            other = (pass_on(other, 1).astype(F32) + partial[spot + 1]).astype(BF16)
        other = swapped(pass_on(other, 1)).astype(F32)
        return pass_on(own, 1).astype(F32) + partial[-1] + other

    residual = (hidden.astype(F32) + ring_sums(partial, first)).astype(BF16)
    normed = rms_scale(residual.astype(F32), norm_gain).astype(BF16)

    def serve(pieces, kinds, digits):
        total = None
        for local in range(local_experts):
            plain = kinds if local_experts == 1 else [F32] * len(kinds)
            served = experts(pieces, plain, digits, own_experts, other_experts, local)
            total = served if local == 0 else [a + b for a, b in zip(total, served)]
        return [part.astype(kind) for part, kind in zip(total, kinds)]

    own, other = normed, swapped(normed)
    pieces = [own]
    for offset in range(1, hops):
        own, other = pass_on(own, -1), pass_on(other, -1)
        pieces = [own, other] + pieces
    pieces = [pass_on(own, -1)] + pieces
    digits = [arrived[offset] for offset in range(hops, -1, -1)]
    total = serve(pieces[:3], kinds[:3], digits[:2]) + serve(pieces[3:], kinds[3:], digits[2:])
    return (residual.astype(F32) + ring_sums(total, pass_on(total[0], 2))).astype(BF16)


def solution(mesh):
    in_specs = (
        P(("groups", "rows"), None),
        P(("groups", "rows"), None, None, None),
        P(("groups", "rows"), None, None, None),
        P(("groups", "rows")),
        P(("groups", "rows"), None),
        P("rows", None),
        P(),
        P("rows", None, None),
        P("rows", None, None),
        P("rows", None, None),
        P(("groups", "rows"), None),
        P(("groups", "rows"), None),
    )
    out_specs = P(("groups", "rows"), None)
    return jax.shard_map(
        on_device, mesh=mesh, in_specs=in_specs, out_specs=out_specs, check_vma=False
    )
```

```python
import functools
import math

import jax
import jax.numpy as jnp
from jax import lax
from jax.experimental import pallas as pl
from jax.experimental.pallas import tpu as pltpu
from jax.sharding import PartitionSpec as P

TOPK = 8
BF16 = jnp.bfloat16
F32 = jnp.float32


gate_scale = 1.0 / 1024.0


def rms_scale(features, norm_gain):
    mean_square = jnp.mean(features * features, axis=-1, keepdims=True)
    return features * lax.rsqrt(mean_square + 1e-06) * norm_gain


def ring_plan(devices):
    chips = devices // 2
    order = list(range(0, chips, 2)) + list(range(chips - 1, 0, -2))
    swap = [(device, device ^ 1) for device in range(devices)]

    def toward(step):
        pairs = []
        for place in range(chips):
            for core in range(2):
                target = order[(place + step * (1 - 2 * core)) % chips]
                pairs.append((2 * order[place] + core, 2 * target + core))
        return pairs

    return order, toward, swap


VMEM = pl.BlockSpec(memory_space=pltpu.VMEM)
SMEM = pl.BlockSpec(memory_space=pltpu.SMEM)


def ring_view(chips):
    me = lax.axis_index("rows")
    chip, core = lax.div(me, 2), lax.rem(me, 2)
    half = lax.div(chip, 2)
    place = jnp.where(lax.rem(chip, 2) == 0, half, chips - 1 - half)

    def chip_at(offset):
        there = lax.rem(place + (1 - 2 * core) * offset + chips, chips)
        return jnp.where(there < chips // 2, 2 * there, 2 * (chips - 1 - there) + 1)

    return chip, core, chip_at


def attend_kernel(
    chips,
    hops,
    chip_experts,
    lengths_ref,
    q_ref,
    k_ref,
    v_ref,
    ids_ref,
    numer_ref,
    *refs,
):
    far_ref, give_ref, own_ref = refs[:3]
    mine_refs, (q_rows, out_rows, tokens) = refs[3 : hops + 2], refs[hops + 2 :]
    step, steps = pl.program_id(0), pl.num_programs(0)
    block, kv_count, cache_len, head_size = k_ref.shape
    rows, feats = q_ref.shape
    heads = feats // head_size
    group = heads // kv_count

    @pl.when(step == 0)
    def _():
        for head in range(heads):
            q_rows[pl.ds(head, rows, stride=heads), :] = q_ref[
                :, head * head_size : (head + 1) * head_size
            ].astype(F32)

    head_of = lax.broadcasted_iota(jnp.int32, (block, heads, cache_len), 1) // group
    slot = lax.broadcasted_iota(jnp.int32, (heads, cache_len), 1)
    first = pl.multiple_of(step * block * heads, block * heads)
    asked = q_rows[pl.ds(first, block * heads), :].astype(BF16)
    scores = [
        lax.dot_general(
            asked[i * heads : (i + 1) * heads],
            k_ref[i].reshape(kv_count * cache_len, head_size),
            (((1,), (1,)), ((), ())),
            preferred_element_type=F32,
        )
        for i in range(block)
    ]
    scores = jnp.stack(scores)
    live = jnp.stack([slot < lengths_ref[step * block + i] for i in range(block)])
    picked = scores[:, :, :cache_len]
    for kv in range(1, kv_count):
        picked = jnp.where(
            head_of == kv, scores[:, :, kv * cache_len : (kv + 1) * cache_len], picked
        )
    picked = jnp.where(live, picked * (1.0 / math.sqrt(head_size)), -1e30)
    weights = jnp.exp(picked - jnp.max(picked, axis=2, keepdims=True))
    shares = weights / jnp.sum(weights, axis=2, keepdims=True)
    spread = jnp.concatenate(
        [jnp.where(head_of == kv, shares, 0.0) for kv in range(kv_count)], axis=2
    ).astype(BF16)
    for i in range(block):
        values = v_ref[i].reshape(kv_count * cache_len, head_size)
        out_rows[pl.ds(first + i * heads, heads), :] = jnp.dot(
            spread[i], values, preferred_element_type=F32
        )

    @pl.when(step == steps - 1)
    def _():
        chip_heads = heads // chips
        chip_feats = chip_heads * head_size
        for head in range(heads):
            start = (head % chip_heads) * head_size
            tokens[head // chip_heads, :, start : start + head_size] = out_rows[
                pl.ds(head, rows, stride=heads), :
            ].astype(BF16)
        extra = tokens.shape[2] - chip_feats
        choices = ids_ref.shape[0]
        total = chips * chip_experts
        expert = lax.broadcasted_iota(jnp.int32, (total, rows), 0)
        found = jnp.zeros((total, rows), jnp.int32)
        for j in range(choices):
            found += jnp.where(ids_ref[j : j + 1, :] == expert, numer_ref[j : j + 1, :], 0)
        digits = jnp.concatenate([found >> 4, found & 15], axis=0).astype(F32).astype(BF16)
        source = lax.broadcasted_iota(jnp.int32, (2 * total, extra), 0)
        lane = lax.broadcasted_iota(jnp.int32, (2 * total, extra), 1)
        for there in range(chips):
            base = there * chip_experts
            wanted = jnp.where(lane < chip_experts, base + lane, total + base + lane - chip_experts)
            pick = (source == wanted) & (lane < 2 * chip_experts)
            tokens[there, :, chip_feats:] = lax.dot_general(
                digits,
                jnp.where(pick, 1.0, 0.0).astype(BF16),
                (((0,), (0,)), ((), ())),
                preferred_element_type=F32,
            ).astype(BF16)
        chip, _, chip_at = ring_view(chips)
        far_ref[...] = tokens[chip_at(-hops)]
        own_ref[...] = tokens[chip]
        for offset in range(1, hops):
            mine_refs[offset - 1][...] = tokens[chip_at(-offset)]
            give_ref[offset - 1] = tokens[chip_at(offset)]


def attend(devices, chip_experts, queries, cache_keys, cache_values, lengths, ids, numer):
    chips, hops = devices // 2, devices // 4
    rows, feats = queries.shape
    kv_count, cache_len, head_size = cache_keys.shape[1:]
    heads = feats // head_size
    extra = -(-2 * chip_experts // 128) * 128
    wide = feats // chips + extra
    block = 32
    cache = pl.BlockSpec((block, kv_count, cache_len, head_size), lambda t: (t, 0, 0, 0))
    one = jax.ShapeDtypeStruct((rows, wide), BF16)
    several = jax.ShapeDtypeStruct((hops - 1, rows, wide), BF16)
    return pl.pallas_call(
        functools.partial(attend_kernel, chips, hops, chip_experts),
        out_shape=(one, several) + (one,) * hops,
        grid=(rows // block,),
        in_specs=[SMEM, VMEM, cache, cache, VMEM, VMEM],
        out_specs=(VMEM,) * (hops + 2),
        scratch_shapes=[
            pltpu.VMEM((rows * heads, head_size), F32),
            pltpu.VMEM((rows * heads, head_size), F32),
            pltpu.VMEM((chips, rows, wide), BF16),
        ],
        compiler_params=pltpu.CompilerParams(vmem_limit_bytes=54 * 1024 * 1024),
        cost_estimate=pl.CostEstimate(
            flops=4 * rows * heads * cache_len * head_size,
            bytes_accessed=4 * rows * kv_count * cache_len * head_size,
            transcendentals=rows * heads * cache_len,
        ),
    )(lengths, queries, cache_keys, cache_values, ids.T, numer.T)


def project_kernel(pieces, kept, *refs):
    piece_refs, own_ref, other_ref = refs[:pieces], refs[pieces], refs[pieces + 1]
    out_refs, x_ref = refs[pieces + 2 : -1], refs[-1]
    if kept:
        out_refs[-1][...] = own_ref[...]
        out_refs = out_refs[:-1]
    feats, width = own_ref.shape
    start = 0
    for piece in piece_refs:
        x_ref[start : start + piece.shape[0], :] = piece[:, : 2 * feats]
        start += piece.shape[0]

    def both(first, second):
        tile = 512
        for column in range(0, width, tile):
            done = jnp.dot(
                x_ref[:, :feats], first[:, column : column + tile], preferred_element_type=F32
            ) + jnp.dot(
                x_ref[:, feats:], second[:, column : column + tile], preferred_element_type=F32
            )
            start = 0
            for out in out_refs:
                out[:, column : column + tile] = done[start : start + out.shape[0]].astype(
                    out.dtype
                )
                start += out.shape[0]

    core = lax.rem(lax.axis_index("rows"), 2)

    @pl.when(core == 0)
    def _():
        both(own_ref, other_ref)

    @pl.when(core == 1)
    def _():
        both(other_ref, own_ref)


def project(pieces, kinds, own, other, kept=False):
    feats, width = own.shape
    rows = sum(piece.shape[0] for piece in pieces)
    return pl.pallas_call(
        functools.partial(project_kernel, len(pieces), kept),
        out_shape=tuple(
            jax.ShapeDtypeStruct((rows // len(kinds), width), kind) for kind in kinds
        )
        + (jax.ShapeDtypeStruct(own.shape, own.dtype),) * kept,
        in_specs=[VMEM] * (len(pieces) + 2),
        out_specs=(VMEM,) * (len(kinds) + kept),
        scratch_shapes=[pltpu.VMEM((rows, 2 * feats), BF16)],
        compiler_params=pltpu.CompilerParams(vmem_limit_bytes=32 * 1024 * 1024),
        cost_estimate=pl.CostEstimate(
            flops=4 * rows * feats * width, bytes_accessed=4 * feats * width, transcendentals=0
        ),
    )(*pieces, own, other)


def expert_kernel(pieces, blocks, local, local_experts, *refs):
    piece_refs, digit_refs, refs = refs[:pieces], refs[pieces : pieces + blocks], refs[pieces + blocks :]
    weight_refs, refs = refs[:6], refs[6:]
    out_refs, (x_ref, inner_ref, gates_ref) = refs[:pieces], refs[pieces:]
    size = piece_refs[0].shape[0]
    for index, piece in enumerate(piece_refs):
        x_ref[index * size : (index + 1) * size, :] = piece[...]
    core = lax.rem(lax.axis_index("rows"), 2)
    chip_experts = 2 * local_experts
    start = 0
    for digits in digit_refs:
        feats = digits.shape[1] - 128 * (-(-2 * chip_experts // 128))
        taken = digits[:, feats:].astype(F32)

        def gate(k):
            high, low = taken[:, k : k + 1], taken[:, chip_experts + k : chip_experts + k + 1]
            return (high * 16.0 + low) * gate_scale

        first, second = gate(local), gate(local_experts + local)
        stop = start + digits.shape[0]
        gates_ref[0, start:stop, :] = jnp.where(core == 0, first, second)
        gates_ref[1, start:stop, :] = jnp.where(core == 0, second, first)
        start = stop
    gates = (gates_ref[0], gates_ref[1])
    hidden_units, width = weight_refs[2].shape[1:]
    tile = 256
    for which in range(2):
        w_gate, w_up = weight_refs[3 * which], weight_refs[3 * which + 1]
        for start in range(0, hidden_units, tile):
            gate_proj = jnp.dot(
                x_ref[...], w_gate[local, :, start : start + tile], preferred_element_type=F32
            )
            raised = jnp.dot(
                x_ref[...], w_up[local, :, start : start + tile], preferred_element_type=F32
            )
            inner = jax.nn.silu(gate_proj) * raised * gates[which]
            place = which * hidden_units + start
            inner_ref[:, place : place + tile] = inner.astype(BF16)
    tile = 512
    for start in range(0, width, tile):
        done = jnp.dot(
            inner_ref[:, :hidden_units],
            weight_refs[2][local, :, start : start + tile],
            preferred_element_type=F32,
        ) + jnp.dot(
            inner_ref[:, hidden_units:],
            weight_refs[5][local, :, start : start + tile],
            preferred_element_type=F32,
        )
        for index, out in enumerate(out_refs):
            out[:, start : start + tile] = done[index * size : (index + 1) * size].astype(
                out.dtype
            )


def experts(pieces, kinds, digits, own, other, local):
    local_experts, width, hidden_units = own[0].shape
    rows = sum(piece.shape[0] for piece in pieces)
    return pl.pallas_call(
        functools.partial(expert_kernel, len(pieces), len(digits), local, local_experts),
        out_shape=tuple(
            jax.ShapeDtypeStruct((piece.shape[0], width), kind)
            for piece, kind in zip(pieces, kinds)
        ),
        in_specs=[VMEM] * (len(pieces) + len(digits) + 6),
        out_specs=(VMEM,) * len(pieces),
        scratch_shapes=[
            pltpu.VMEM((rows, width), BF16),
            pltpu.VMEM((rows, 2 * hidden_units), BF16),
            pltpu.VMEM((2, rows, 1), F32),
        ],
        compiler_params=pltpu.CompilerParams(vmem_limit_bytes=16 * 1024 * 1024),
        cost_estimate=pl.CostEstimate(
            flops=12 * rows * hidden_units * width,
            bytes_accessed=rows * width,
            transcendentals=2 * rows * hidden_units,
        ),
    )(*pieces, *digits, *own, *other)


def on_device(
    queries,
    cache_keys,
    cache_values,
    lengths,
    hidden,
    out_weight,
    norm_gain,
    w_gate,
    w_up,
    w_down,
    expert_ids,
    gate_numer,
):
    devices = lax.axis_size("rows")
    hops = devices // 4
    local_experts = w_gate.shape[0]
    order, toward, swap = ring_plan(devices)

    def pass_on(array, step):
        return lax.ppermute(array, "rows", toward(step))

    def swapped(array):
        return lax.ppermute(array, "rows", swap)

    weight_other = swapped(out_weight)
    own_experts = (w_gate, w_up, w_down)

    far, give, here, *mine = attend(
        devices,
        2 * local_experts,
        queries,
        cache_keys,
        cache_values,
        lengths,
        expert_ids,
        gate_numer,
    )
    got = swapped(give)

    def send(offset, mine, got):
        return pass_on(jnp.concatenate([mine, got], axis=0), -offset)

    kinds = [BF16, BF16, BF16] + [F32] * (2 * hops - 3)
    arrived = {0: here, hops: pass_on(far, -hops)}
    arrived[hops - 1] = send(hops - 1, mine[hops - 2], got[hops - 2])
    *partial, own_weight = project([arrived[hops]], kinds[:1], out_weight, weight_other, True)
    weights = (own_weight, weight_other)
    partial += project([arrived[hops - 1]], kinds[1:3], *weights)
    first = pass_on(partial[0], 2)
    first, own_experts = lax.optimization_barrier((first, own_experts))
    for offset in range(hops - 2, 0, -1):
        arrived[offset] = send(offset, mine[offset - 1], got[offset - 1])
    nearer = [arrived[offset] for offset in range(hops - 2, 0, -1)]
    partial += project(nearer, kinds[3:-1], *weights)
    partial += project([here], kinds[-1:], *weights)
    _, own_experts = lax.optimization_barrier((partial, own_experts))
    other_experts = tuple(swapped(w) for w in own_experts)

    def ring_sums(partial, far):
        own, other = partial[1].astype(BF16), partial[2]
        for offset in range(hops - 2, 0, -1):
            spot = 1 + 2 * (hops - 1 - offset)
            own = pass_on(own, 1).astype(F32) + partial[spot]
            if offset == hops - 2:
                own = own + far.astype(F32)
            own = own.astype(BF16)
            other = (pass_on(other, 1).astype(F32) + partial[spot + 1]).astype(BF16)
        other = swapped(pass_on(other, 1)).astype(F32)
        return pass_on(own, 1).astype(F32) + partial[-1] + other

    residual = (hidden.astype(F32) + ring_sums(partial, first)).astype(BF16)
    normed = rms_scale(residual.astype(F32), norm_gain).astype(BF16)

    def serve(pieces, kinds, digits):
        total = None
        for local in range(local_experts):
            plain = kinds if local_experts == 1 else [F32] * len(kinds)
            served = experts(pieces, plain, digits, own_experts, other_experts, local)
            total = served if local == 0 else [a + b for a, b in zip(total, served)]
        return [part.astype(kind) for part, kind in zip(total, kinds)]

    own, other = normed, swapped(normed)
    pieces = [own]
    for offset in range(1, hops):
        own, other = pass_on(own, -1), pass_on(other, -1)
        pieces = [own, other] + pieces
    pieces = [pass_on(own, -1)] + pieces
    digits = [arrived[offset] for offset in range(hops, -1, -1)]
    nearer = serve(pieces[3:], kinds[3:], digits[2:])
    pieces[2], nearer = lax.optimization_barrier((pieces[2], nearer))
    total = serve(pieces[:3], kinds[:3], digits[:2]) + nearer
    return (residual.astype(F32) + ring_sums(total, pass_on(total[0], 2))).astype(BF16)


def solution(mesh):
    in_specs = (
        P(("groups", "rows"), None),
        P(("groups", "rows"), None, None, None),
        P(("groups", "rows"), None, None, None),
        P(("groups", "rows")),
        P(("groups", "rows"), None),
        P("rows", None),
        P(),
        P("rows", None, None),
        P("rows", None, None),
        P("rows", None, None),
        P(("groups", "rows"), None),
        P(("groups", "rows"), None),
    )
    out_specs = P(("groups", "rows"), None)
    return jax.shard_map(
        on_device, mesh=mesh, in_specs=in_specs, out_specs=out_specs, check_vma=False
    )
```

```python
import functools
import math

import jax
import jax.numpy as jnp
from jax import lax
from jax.experimental import pallas as pl
from jax.experimental.pallas import tpu as pltpu
from jax.sharding import PartitionSpec as P

TOPK = 8
BF16 = jnp.bfloat16
F32 = jnp.float32


gate_scale = 1.0 / 1024.0


def rms_scale(features, norm_gain):
    mean_square = jnp.mean(features * features, axis=-1, keepdims=True)
    return features * lax.rsqrt(mean_square + 1e-06) * norm_gain


def ring_plan(devices):
    chips = devices // 2
    order = list(range(0, chips, 2)) + list(range(chips - 1, 0, -2))
    swap = [(device, device ^ 1) for device in range(devices)]

    def toward(step):
        pairs = []
        for place in range(chips):
            for core in range(2):
                target = order[(place + step * (1 - 2 * core)) % chips]
                pairs.append((2 * order[place] + core, 2 * target + core))
        return pairs

    return order, toward, swap


VMEM = pl.BlockSpec(memory_space=pltpu.VMEM)
SMEM = pl.BlockSpec(memory_space=pltpu.SMEM)


def ring_view(chips):
    me = lax.axis_index("rows")
    chip, core = lax.div(me, 2), lax.rem(me, 2)
    half = lax.div(chip, 2)
    place = jnp.where(lax.rem(chip, 2) == 0, half, chips - 1 - half)

    def chip_at(offset):
        there = lax.rem(place + (1 - 2 * core) * offset + chips, chips)
        return jnp.where(there < chips // 2, 2 * there, 2 * (chips - 1 - there) + 1)

    return chip, core, chip_at


def attend_kernel(
    chips,
    hops,
    chip_experts,
    lengths_ref,
    q_ref,
    k_ref,
    v_ref,
    ids_ref,
    numer_ref,
    *refs,
):
    far_ref, give_ref, own_ref = refs[:3]
    mine_refs, (q_rows, out_rows, tokens) = refs[3 : hops + 2], refs[hops + 2 :]
    step, steps = pl.program_id(0), pl.num_programs(0)
    block, kv_count, cache_len, head_size = k_ref.shape
    rows, feats = q_ref.shape
    heads = feats // head_size
    group = heads // kv_count

    @pl.when(step == 0)
    def _():
        for head in range(heads):
            q_rows[pl.ds(head, rows, stride=heads), :] = q_ref[
                :, head * head_size : (head + 1) * head_size
            ].astype(F32)

    head_of = lax.broadcasted_iota(jnp.int32, (block, heads, cache_len), 1) // group
    slot = lax.broadcasted_iota(jnp.int32, (heads, cache_len), 1)
    first = pl.multiple_of(step * block * heads, block * heads)
    asked = q_rows[pl.ds(first, block * heads), :].astype(BF16)
    scores = [
        lax.dot_general(
            asked[i * heads : (i + 1) * heads],
            k_ref[i].reshape(kv_count * cache_len, head_size),
            (((1,), (1,)), ((), ())),
            preferred_element_type=F32,
        )
        for i in range(block)
    ]
    scores = jnp.stack(scores)
    live = jnp.stack([slot < lengths_ref[step * block + i] for i in range(block)])
    picked = scores[:, :, :cache_len]
    for kv in range(1, kv_count):
        picked = jnp.where(
            head_of == kv, scores[:, :, kv * cache_len : (kv + 1) * cache_len], picked
        )
    picked = jnp.where(live, picked * (1.0 / math.sqrt(head_size)), -1e30)
    weights = jnp.exp(picked - jnp.max(picked, axis=2, keepdims=True))
    shares = weights / jnp.sum(weights, axis=2, keepdims=True)
    spread = jnp.concatenate(
        [jnp.where(head_of == kv, shares, 0.0) for kv in range(kv_count)], axis=2
    ).astype(BF16)
    for i in range(block):
        values = v_ref[i].reshape(kv_count * cache_len, head_size)
        out_rows[pl.ds(first + i * heads, heads), :] = jnp.dot(
            spread[i], values, preferred_element_type=F32
        )

    @pl.when(step == steps - 1)
    def _():
        chip_heads = heads // chips
        chip_feats = chip_heads * head_size
        for head in range(heads):
            start = (head % chip_heads) * head_size
            tokens[head // chip_heads, :, start : start + head_size] = out_rows[
                pl.ds(head, rows, stride=heads), :
            ].astype(BF16)
        extra = tokens.shape[2] - chip_feats
        choices = ids_ref.shape[0]
        total = chips * chip_experts
        expert = lax.broadcasted_iota(jnp.int32, (total, rows), 0)
        found = jnp.zeros((total, rows), jnp.int32)
        for j in range(choices):
            found += jnp.where(ids_ref[j : j + 1, :] == expert, numer_ref[j : j + 1, :], 0)
        digits = jnp.concatenate([found >> 4, found & 15], axis=0).astype(F32).astype(BF16)
        source = lax.broadcasted_iota(jnp.int32, (2 * total, extra), 0)
        lane = lax.broadcasted_iota(jnp.int32, (2 * total, extra), 1)
        for there in range(chips):
            base = there * chip_experts
            wanted = jnp.where(lane < chip_experts, base + lane, total + base + lane - chip_experts)
            pick = (source == wanted) & (lane < 2 * chip_experts)
            tokens[there, :, chip_feats:] = lax.dot_general(
                digits,
                jnp.where(pick, 1.0, 0.0).astype(BF16),
                (((0,), (0,)), ((), ())),
                preferred_element_type=F32,
            ).astype(BF16)
        chip, _, chip_at = ring_view(chips)
        far_ref[...] = tokens[chip_at(-hops)]
        own_ref[...] = tokens[chip]
        for offset in range(1, hops):
            mine_refs[offset - 1][...] = tokens[chip_at(-offset)]
            give_ref[offset - 1] = tokens[chip_at(offset)]


def attend(devices, chip_experts, queries, cache_keys, cache_values, lengths, ids, numer):
    chips, hops = devices // 2, devices // 4
    rows, feats = queries.shape
    kv_count, cache_len, head_size = cache_keys.shape[1:]
    heads = feats // head_size
    extra = -(-2 * chip_experts // 128) * 128
    wide = feats // chips + extra
    block = 32
    cache = pl.BlockSpec((block, kv_count, cache_len, head_size), lambda t: (t, 0, 0, 0))
    one = jax.ShapeDtypeStruct((rows, wide), BF16)
    several = jax.ShapeDtypeStruct((hops - 1, rows, wide), BF16)
    return pl.pallas_call(
        functools.partial(attend_kernel, chips, hops, chip_experts),
        out_shape=(one, several) + (one,) * hops,
        grid=(rows // block,),
        in_specs=[SMEM, VMEM, cache, cache, VMEM, VMEM],
        out_specs=(VMEM,) * (hops + 2),
        scratch_shapes=[
            pltpu.VMEM((rows * heads, head_size), F32),
            pltpu.VMEM((rows * heads, head_size), F32),
            pltpu.VMEM((chips, rows, wide), BF16),
        ],
        compiler_params=pltpu.CompilerParams(vmem_limit_bytes=54 * 1024 * 1024),
        cost_estimate=pl.CostEstimate(
            flops=4 * rows * heads * cache_len * head_size,
            bytes_accessed=4 * rows * kv_count * cache_len * head_size,
            transcendentals=rows * heads * cache_len,
        ),
    )(lengths, queries, cache_keys, cache_values, ids.T, numer.T)


def project_kernel(pieces, kept, *refs):
    piece_refs, own_ref, other_ref = refs[:pieces], refs[pieces], refs[pieces + 1]
    out_refs, x_ref = refs[pieces + 2 : -1], refs[-1]
    if kept:
        out_refs[-1][...] = own_ref[...]
        out_refs = out_refs[:-1]
    feats, width = own_ref.shape
    start = 0
    for piece in piece_refs:
        x_ref[start : start + piece.shape[0], :] = piece[:, : 2 * feats]
        start += piece.shape[0]

    def both(first, second):
        tile = 512
        for column in range(0, width, tile):
            done = jnp.dot(
                x_ref[:, :feats], first[:, column : column + tile], preferred_element_type=F32
            ) + jnp.dot(
                x_ref[:, feats:], second[:, column : column + tile], preferred_element_type=F32
            )
            start = 0
            for out in out_refs:
                out[:, column : column + tile] = done[start : start + out.shape[0]].astype(
                    out.dtype
                )
                start += out.shape[0]

    core = lax.rem(lax.axis_index("rows"), 2)

    @pl.when(core == 0)
    def _():
        both(own_ref, other_ref)

    @pl.when(core == 1)
    def _():
        both(other_ref, own_ref)


def project(pieces, kinds, own, other, kept=False):
    feats, width = own.shape
    rows = sum(piece.shape[0] for piece in pieces)
    return pl.pallas_call(
        functools.partial(project_kernel, len(pieces), kept),
        out_shape=tuple(
            jax.ShapeDtypeStruct((rows // len(kinds), width), kind) for kind in kinds
        )
        + (jax.ShapeDtypeStruct(own.shape, own.dtype),) * kept,
        in_specs=[VMEM] * (len(pieces) + 2),
        out_specs=(VMEM,) * (len(kinds) + kept),
        scratch_shapes=[pltpu.VMEM((rows, 2 * feats), BF16)],
        compiler_params=pltpu.CompilerParams(vmem_limit_bytes=32 * 1024 * 1024),
        cost_estimate=pl.CostEstimate(
            flops=4 * rows * feats * width, bytes_accessed=4 * feats * width, transcendentals=0
        ),
    )(*pieces, own, other)


def expert_kernel(pieces, blocks, local, local_experts, *refs):
    piece_refs, digit_refs, refs = refs[:pieces], refs[pieces : pieces + blocks], refs[pieces + blocks :]
    weight_refs, refs = refs[:6], refs[6:]
    out_refs, (x_ref, inner_ref, gates_ref) = refs[:pieces], refs[pieces:]
    size = piece_refs[0].shape[0]
    for index, piece in enumerate(piece_refs):
        x_ref[index * size : (index + 1) * size, :] = piece[...]
    core = lax.rem(lax.axis_index("rows"), 2)
    chip_experts = 2 * local_experts
    start = 0
    for digits in digit_refs:
        feats = digits.shape[1] - 128 * (-(-2 * chip_experts // 128))
        taken = digits[:, feats:].astype(F32)

        def gate(k):
            high, low = taken[:, k : k + 1], taken[:, chip_experts + k : chip_experts + k + 1]
            return (high * 16.0 + low) * gate_scale

        first, second = gate(local), gate(local_experts + local)
        stop = start + digits.shape[0]
        gates_ref[0, start:stop, :] = jnp.where(core == 0, first, second)
        gates_ref[1, start:stop, :] = jnp.where(core == 0, second, first)
        start = stop
    gates = (gates_ref[0], gates_ref[1])
    hidden_units, width = weight_refs[2].shape[1:]
    tile = 256
    for which in range(2):
        w_gate, w_up = weight_refs[3 * which], weight_refs[3 * which + 1]
        for start in range(0, hidden_units, tile):
            gate_proj = jnp.dot(
                x_ref[...], w_gate[local, :, start : start + tile], preferred_element_type=F32
            )
            raised = jnp.dot(
                x_ref[...], w_up[local, :, start : start + tile], preferred_element_type=F32
            )
            inner = jax.nn.silu(gate_proj) * raised * gates[which]
            place = which * hidden_units + start
            inner_ref[:, place : place + tile] = inner.astype(BF16)
    tile = 512
    for start in range(0, width, tile):
        done = jnp.dot(
            inner_ref[:, :hidden_units],
            weight_refs[2][local, :, start : start + tile],
            preferred_element_type=F32,
        ) + jnp.dot(
            inner_ref[:, hidden_units:],
            weight_refs[5][local, :, start : start + tile],
            preferred_element_type=F32,
        )
        for index, out in enumerate(out_refs):
            out[:, start : start + tile] = done[index * size : (index + 1) * size].astype(
                out.dtype
            )


def experts(pieces, kinds, digits, own, other, local):
    local_experts, width, hidden_units = own[0].shape
    rows = sum(piece.shape[0] for piece in pieces)
    return pl.pallas_call(
        functools.partial(expert_kernel, len(pieces), len(digits), local, local_experts),
        out_shape=tuple(
            jax.ShapeDtypeStruct((piece.shape[0], width), kind)
            for piece, kind in zip(pieces, kinds)
        ),
        in_specs=[VMEM] * (len(pieces) + len(digits) + 6),
        out_specs=(VMEM,) * len(pieces),
        scratch_shapes=[
            pltpu.VMEM((rows, width), BF16),
            pltpu.VMEM((rows, 2 * hidden_units), BF16),
            pltpu.VMEM((2, rows, 1), F32),
        ],
        compiler_params=pltpu.CompilerParams(vmem_limit_bytes=16 * 1024 * 1024),
        cost_estimate=pl.CostEstimate(
            flops=12 * rows * hidden_units * width,
            bytes_accessed=rows * width,
            transcendentals=2 * rows * hidden_units,
        ),
    )(*pieces, *digits, *own, *other)


def on_device(
    queries,
    cache_keys,
    cache_values,
    lengths,
    hidden,
    out_weight,
    norm_gain,
    w_gate,
    w_up,
    w_down,
    expert_ids,
    gate_numer,
):
    devices = lax.axis_size("rows")
    hops = devices // 4
    local_experts = w_gate.shape[0]
    order, toward, swap = ring_plan(devices)

    def pass_on(array, step):
        return lax.ppermute(array, "rows", toward(step))

    def swapped(array):
        return lax.ppermute(array, "rows", swap)

    weight_other = swapped(out_weight)
    own_experts = (w_gate, w_up, w_down)

    far, give, here, *mine = attend(
        devices,
        2 * local_experts,
        queries,
        cache_keys,
        cache_values,
        lengths,
        expert_ids,
        gate_numer,
    )
    got = swapped(give)

    def send(offset, mine, got):
        return pass_on(jnp.concatenate([mine, got], axis=0), -offset)

    kinds = [BF16, BF16, BF16] + [F32] * (2 * hops - 3)
    arrived = {0: here, hops: pass_on(far, -hops)}
    arrived[hops - 1] = send(hops - 1, mine[hops - 2], got[hops - 2])
    *partial, own_weight = project([arrived[hops]], kinds[:1], out_weight, weight_other, True)
    weights = (own_weight, weight_other)
    partial += project([arrived[hops - 1]], kinds[1:3], *weights)
    first = pass_on(partial[0], 2)
    first, own_experts = lax.optimization_barrier((first, own_experts))
    for offset in range(hops - 2, 0, -1):
        arrived[offset] = send(offset, mine[offset - 1], got[offset - 1])
    for offset in range(hops - 2, 0, -1):
        partial += project([arrived[offset]], kinds[3:5], *weights)
    partial += project([here], kinds[-1:], *weights)
    _, own_experts = lax.optimization_barrier((partial, own_experts))
    other_experts = tuple(swapped(w) for w in own_experts)

    def ring_sums(partial, far):
        own, other = partial[1].astype(BF16), partial[2]
        for offset in range(hops - 2, 0, -1):
            spot = 1 + 2 * (hops - 1 - offset)
            own = pass_on(own, 1).astype(F32) + partial[spot]
            if offset == hops - 2:
                own = own + far.astype(F32)
            own = own.astype(BF16)
            other = (pass_on(other, 1).astype(F32) + partial[spot + 1]).astype(BF16)
        other = swapped(pass_on(other, 1)).astype(F32)
        return pass_on(own, 1).astype(F32) + partial[-1] + other

    residual = (hidden.astype(F32) + ring_sums(partial, first)).astype(BF16)
    normed = rms_scale(residual.astype(F32), norm_gain).astype(BF16)

    def serve(pieces, kinds, digits):
        total = None
        for local in range(local_experts):
            plain = kinds if local_experts == 1 else [F32] * len(kinds)
            served = experts(pieces, plain, digits, own_experts, other_experts, local)
            total = served if local == 0 else [a + b for a, b in zip(total, served)]
        return [part.astype(kind) for part, kind in zip(total, kinds)]

    own, other = normed, swapped(normed)
    pieces = [own]
    for offset in range(1, hops):
        own, other = pass_on(own, -1), pass_on(other, -1)
        pieces = [own, other] + pieces
    pieces = [pass_on(own, -1)] + pieces
    digits = [arrived[offset] for offset in range(hops, -1, -1)]
    nearer = serve(pieces[3:], kinds[3:], digits[2:])
    pieces[1], pieces[2], nearer = lax.optimization_barrier((pieces[1], pieces[2], nearer))
    total = serve(pieces[:3], kinds[:3], digits[:2]) + nearer
    return (residual.astype(F32) + ring_sums(total, pass_on(total[0], 2))).astype(BF16)


def solution(mesh):
    in_specs = (
        P(("groups", "rows"), None),
        P(("groups", "rows"), None, None, None),
        P(("groups", "rows"), None, None, None),
        P(("groups", "rows")),
        P(("groups", "rows"), None),
        P("rows", None),
        P(),
        P("rows", None, None),
        P("rows", None, None),
        P("rows", None, None),
        P(("groups", "rows"), None),
        P(("groups", "rows"), None),
    )
    out_specs = P(("groups", "rows"), None)
    return jax.shard_map(
        on_device, mesh=mesh, in_specs=in_specs, out_specs=out_specs, check_vma=False
    )
```

```python
import functools
import math

import jax
import jax.numpy as jnp
from jax import lax
from jax.experimental import pallas as pl
from jax.experimental.pallas import tpu as pltpu
from jax.sharding import PartitionSpec as P

TOPK = 8
BF16 = jnp.bfloat16
F32 = jnp.float32


gate_scale = 1.0 / 1024.0


def rms_scale(features, norm_gain):
    mean_square = jnp.mean(features * features, axis=-1, keepdims=True)
    return features * lax.rsqrt(mean_square + 1e-06) * norm_gain


def ring_plan(devices):
    chips = devices // 2
    order = list(range(0, chips, 2)) + list(range(chips - 1, 0, -2))
    swap = [(device, device ^ 1) for device in range(devices)]

    def toward(step):
        pairs = []
        for place in range(chips):
            for core in range(2):
                target = order[(place + step * (1 - 2 * core)) % chips]
                pairs.append((2 * order[place] + core, 2 * target + core))
        return pairs

    return order, toward, swap


VMEM = pl.BlockSpec(memory_space=pltpu.VMEM)
SMEM = pl.BlockSpec(memory_space=pltpu.SMEM)


def ring_view(chips):
    me = lax.axis_index("rows")
    chip, core = lax.div(me, 2), lax.rem(me, 2)
    half = lax.div(chip, 2)
    place = jnp.where(lax.rem(chip, 2) == 0, half, chips - 1 - half)

    def chip_at(offset):
        there = lax.rem(place + (1 - 2 * core) * offset + chips, chips)
        return jnp.where(there < chips // 2, 2 * there, 2 * (chips - 1 - there) + 1)

    return chip, core, chip_at


def attend_kernel(
    chips,
    hops,
    chip_experts,
    lengths_ref,
    q_ref,
    k_ref,
    v_ref,
    ids_ref,
    numer_ref,
    *refs,
):
    far_ref, give_ref, own_ref = refs[:3]
    mine_refs, (q_rows, out_rows, tokens) = refs[3 : hops + 2], refs[hops + 2 :]
    step, steps = pl.program_id(0), pl.num_programs(0)
    block, kv_count, cache_len, head_size = k_ref.shape
    rows, feats = q_ref.shape
    heads = feats // head_size
    group = heads // kv_count

    @pl.when(step == 0)
    def _():
        for head in range(heads):
            q_rows[pl.ds(head, rows, stride=heads), :] = q_ref[
                :, head * head_size : (head + 1) * head_size
            ].astype(F32)

    head_of = lax.broadcasted_iota(jnp.int32, (block, heads, cache_len), 1) // group
    slot = lax.broadcasted_iota(jnp.int32, (heads, cache_len), 1)
    first = pl.multiple_of(step * block * heads, block * heads)
    asked = q_rows[pl.ds(first, block * heads), :].astype(BF16)
    scores = [
        lax.dot_general(
            asked[i * heads : (i + 1) * heads],
            k_ref[i].reshape(kv_count * cache_len, head_size),
            (((1,), (1,)), ((), ())),
            preferred_element_type=F32,
        )
        for i in range(block)
    ]
    scores = jnp.stack(scores)
    live = jnp.stack([slot < lengths_ref[step * block + i] for i in range(block)])
    picked = scores[:, :, :cache_len]
    for kv in range(1, kv_count):
        picked = jnp.where(
            head_of == kv, scores[:, :, kv * cache_len : (kv + 1) * cache_len], picked
        )
    picked = jnp.where(live, picked * (1.0 / math.sqrt(head_size)), -1e30)
    weights = jnp.exp(picked - jnp.max(picked, axis=2, keepdims=True))
    shares = weights / jnp.sum(weights, axis=2, keepdims=True)
    spread = jnp.concatenate(
        [jnp.where(head_of == kv, shares, 0.0) for kv in range(kv_count)], axis=2
    ).astype(BF16)
    for i in range(block):
        values = v_ref[i].reshape(kv_count * cache_len, head_size)
        out_rows[pl.ds(first + i * heads, heads), :] = jnp.dot(
            spread[i], values, preferred_element_type=F32
        )

    @pl.when(step == steps - 1)
    def _():
        chip_heads = heads // chips
        chip_feats = chip_heads * head_size
        for head in range(heads):
            start = (head % chip_heads) * head_size
            tokens[head // chip_heads, :, start : start + head_size] = out_rows[
                pl.ds(head, rows, stride=heads), :
            ].astype(BF16)
        extra = tokens.shape[2] - chip_feats
        choices = ids_ref.shape[0]
        total = chips * chip_experts
        expert = lax.broadcasted_iota(jnp.int32, (total, rows), 0)
        found = jnp.zeros((total, rows), jnp.int32)
        for j in range(choices):
            found += jnp.where(ids_ref[j : j + 1, :] == expert, numer_ref[j : j + 1, :], 0)
        digits = jnp.concatenate([found >> 4, found & 15], axis=0).astype(F32).astype(BF16)
        source = lax.broadcasted_iota(jnp.int32, (2 * total, extra), 0)
        lane = lax.broadcasted_iota(jnp.int32, (2 * total, extra), 1)
        for there in range(chips):
            base = there * chip_experts
            wanted = jnp.where(lane < chip_experts, base + lane, total + base + lane - chip_experts)
            pick = (source == wanted) & (lane < 2 * chip_experts)
            tokens[there, :, chip_feats:] = lax.dot_general(
                digits,
                jnp.where(pick, 1.0, 0.0).astype(BF16),
                (((0,), (0,)), ((), ())),
                preferred_element_type=F32,
            ).astype(BF16)
        chip, _, chip_at = ring_view(chips)
        far_ref[...] = tokens[chip_at(-hops)]
        own_ref[...] = tokens[chip]
        for offset in range(1, hops):
            mine_refs[offset - 1][...] = tokens[chip_at(-offset)]
            give_ref[offset - 1] = tokens[chip_at(offset)]


def attend(devices, chip_experts, queries, cache_keys, cache_values, lengths, ids, numer):
    chips, hops = devices // 2, devices // 4
    rows, feats = queries.shape
    kv_count, cache_len, head_size = cache_keys.shape[1:]
    heads = feats // head_size
    extra = -(-2 * chip_experts // 128) * 128
    wide = feats // chips + extra
    block = 32
    cache = pl.BlockSpec((block, kv_count, cache_len, head_size), lambda t: (t, 0, 0, 0))
    one = jax.ShapeDtypeStruct((rows, wide), BF16)
    several = jax.ShapeDtypeStruct((hops - 1, rows, wide), BF16)
    return pl.pallas_call(
        functools.partial(attend_kernel, chips, hops, chip_experts),
        out_shape=(one, several) + (one,) * hops,
        grid=(rows // block,),
        in_specs=[SMEM, VMEM, cache, cache, VMEM, VMEM],
        out_specs=(VMEM,) * (hops + 2),
        scratch_shapes=[
            pltpu.VMEM((rows * heads, head_size), F32),
            pltpu.VMEM((rows * heads, head_size), F32),
            pltpu.VMEM((chips, rows, wide), BF16),
        ],
        compiler_params=pltpu.CompilerParams(vmem_limit_bytes=54 * 1024 * 1024),
        cost_estimate=pl.CostEstimate(
            flops=4 * rows * heads * cache_len * head_size,
            bytes_accessed=4 * rows * kv_count * cache_len * head_size,
            transcendentals=rows * heads * cache_len,
        ),
    )(lengths, queries, cache_keys, cache_values, ids.T, numer.T)


def project_kernel(pieces, kept, *refs):
    piece_refs, own_ref, other_ref = refs[:pieces], refs[pieces], refs[pieces + 1]
    out_refs, x_ref = refs[pieces + 2 : -1], refs[-1]
    if kept:
        out_refs[-1][...] = own_ref[...]
        out_refs = out_refs[:-1]
    feats, width = own_ref.shape
    start = 0
    for piece in piece_refs:
        x_ref[start : start + piece.shape[0], :] = piece[:, : 2 * feats]
        start += piece.shape[0]

    def both(first, second):
        tile = 512
        for column in range(0, width, tile):
            done = jnp.dot(
                x_ref[:, :feats], first[:, column : column + tile], preferred_element_type=F32
            ) + jnp.dot(
                x_ref[:, feats:], second[:, column : column + tile], preferred_element_type=F32
            )
            start = 0
            for out in out_refs:
                out[:, column : column + tile] = done[start : start + out.shape[0]].astype(
                    out.dtype
                )
                start += out.shape[0]

    core = lax.rem(lax.axis_index("rows"), 2)

    @pl.when(core == 0)
    def _():
        both(own_ref, other_ref)

    @pl.when(core == 1)
    def _():
        both(other_ref, own_ref)


def project(pieces, kinds, own, other, kept=False):
    feats, width = own.shape
    rows = sum(piece.shape[0] for piece in pieces)
    return pl.pallas_call(
        functools.partial(project_kernel, len(pieces), kept),
        out_shape=tuple(
            jax.ShapeDtypeStruct((rows // len(kinds), width), kind) for kind in kinds
        )
        + (jax.ShapeDtypeStruct(own.shape, own.dtype),) * kept,
        in_specs=[VMEM] * (len(pieces) + 2),
        out_specs=(VMEM,) * (len(kinds) + kept),
        scratch_shapes=[pltpu.VMEM((rows, 2 * feats), BF16)],
        compiler_params=pltpu.CompilerParams(vmem_limit_bytes=32 * 1024 * 1024),
        cost_estimate=pl.CostEstimate(flops=rows, bytes_accessed=rows, transcendentals=0),
    )(*pieces, own, other)


def expert_kernel(pieces, blocks, local, local_experts, *refs):
    piece_refs, digit_refs, refs = refs[:pieces], refs[pieces : pieces + blocks], refs[pieces + blocks :]
    weight_refs, refs = refs[:6], refs[6:]
    out_refs, (x_ref, inner_ref, gates_ref) = refs[:pieces], refs[pieces:]
    size = piece_refs[0].shape[0]
    for index, piece in enumerate(piece_refs):
        x_ref[index * size : (index + 1) * size, :] = piece[...]
    core = lax.rem(lax.axis_index("rows"), 2)
    chip_experts = 2 * local_experts
    start = 0
    for digits in digit_refs:
        feats = digits.shape[1] - 128 * (-(-2 * chip_experts // 128))
        taken = digits[:, feats:].astype(F32)

        def gate(k):
            high, low = taken[:, k : k + 1], taken[:, chip_experts + k : chip_experts + k + 1]
            return (high * 16.0 + low) * gate_scale

        first, second = gate(local), gate(local_experts + local)
        stop = start + digits.shape[0]
        gates_ref[0, start:stop, :] = jnp.where(core == 0, first, second)
        gates_ref[1, start:stop, :] = jnp.where(core == 0, second, first)
        start = stop
    gates = (gates_ref[0], gates_ref[1])
    hidden_units, width = weight_refs[2].shape[1:]
    tile = 256
    for which in range(2):
        w_gate, w_up = weight_refs[3 * which], weight_refs[3 * which + 1]
        for start in range(0, hidden_units, tile):
            gate_proj = jnp.dot(
                x_ref[...], w_gate[local, :, start : start + tile], preferred_element_type=F32
            )
            raised = jnp.dot(
                x_ref[...], w_up[local, :, start : start + tile], preferred_element_type=F32
            )
            inner = jax.nn.silu(gate_proj) * raised * gates[which]
            place = which * hidden_units + start
            inner_ref[:, place : place + tile] = inner.astype(BF16)
    tile = 512
    for start in range(0, width, tile):
        done = jnp.dot(
            inner_ref[:, :hidden_units],
            weight_refs[2][local, :, start : start + tile],
            preferred_element_type=F32,
        ) + jnp.dot(
            inner_ref[:, hidden_units:],
            weight_refs[5][local, :, start : start + tile],
            preferred_element_type=F32,
        )
        for index, out in enumerate(out_refs):
            out[:, start : start + tile] = done[index * size : (index + 1) * size].astype(
                out.dtype
            )


def experts(pieces, kinds, digits, own, other, local):
    local_experts, width, hidden_units = own[0].shape
    rows = sum(piece.shape[0] for piece in pieces)
    return pl.pallas_call(
        functools.partial(expert_kernel, len(pieces), len(digits), local, local_experts),
        out_shape=tuple(
            jax.ShapeDtypeStruct((piece.shape[0], width), kind)
            for piece, kind in zip(pieces, kinds)
        ),
        in_specs=[VMEM] * (len(pieces) + len(digits) + 6),
        out_specs=(VMEM,) * len(pieces),
        scratch_shapes=[
            pltpu.VMEM((rows, width), BF16),
            pltpu.VMEM((rows, 2 * hidden_units), BF16),
            pltpu.VMEM((2, rows, 1), F32),
        ],
        compiler_params=pltpu.CompilerParams(vmem_limit_bytes=16 * 1024 * 1024),
        cost_estimate=pl.CostEstimate(
            flops=12 * rows * hidden_units * width,
            bytes_accessed=rows * width,
            transcendentals=2 * rows * hidden_units,
        ),
    )(*pieces, *digits, *own, *other)


def on_device(
    queries,
    cache_keys,
    cache_values,
    lengths,
    hidden,
    out_weight,
    norm_gain,
    w_gate,
    w_up,
    w_down,
    expert_ids,
    gate_numer,
):
    devices = lax.axis_size("rows")
    hops = devices // 4
    local_experts = w_gate.shape[0]
    order, toward, swap = ring_plan(devices)

    def pass_on(array, step):
        return lax.ppermute(array, "rows", toward(step))

    def swapped(array):
        return lax.ppermute(array, "rows", swap)

    weight_other = swapped(out_weight)
    own_experts = (w_gate, w_up, w_down)

    far, give, here, *mine = attend(
        devices,
        2 * local_experts,
        queries,
        cache_keys,
        cache_values,
        lengths,
        expert_ids,
        gate_numer,
    )
    got = swapped(give)

    def send(offset, mine, got):
        return pass_on(jnp.concatenate([mine, got], axis=0), -offset)

    kinds = [BF16, BF16, BF16] + [F32] * (2 * hops - 3)
    arrived = {0: here, hops: pass_on(far, -hops)}
    arrived[hops - 1] = send(hops - 1, mine[hops - 2], got[hops - 2])
    *partial, own_weight = project([arrived[hops]], kinds[:1], out_weight, weight_other, True)
    weights = (own_weight, weight_other)
    partial += project([arrived[hops - 1]], kinds[1:3], *weights)
    first = pass_on(partial[0], 2)
    first, own_experts = lax.optimization_barrier((first, own_experts))
    for offset in range(hops - 2, 0, -1):
        arrived[offset] = send(offset, mine[offset - 1], got[offset - 1])
    for offset in range(hops - 2, 0, -1):
        partial += project([arrived[offset]], kinds[3:5], *weights)
    partial += project([here], kinds[-1:], *weights)
    _, own_experts = lax.optimization_barrier((partial, own_experts))
    other_experts = tuple(swapped(w) for w in own_experts)

    def ring_sums(partial, far):
        own, other = partial[1].astype(BF16), partial[2]
        for offset in range(hops - 2, 0, -1):
            spot = 1 + 2 * (hops - 1 - offset)
            own = pass_on(own, 1).astype(F32) + partial[spot]
            if offset == hops - 2:
                own = own + far.astype(F32)
            own = own.astype(BF16)
            other = (pass_on(other, 1).astype(F32) + partial[spot + 1]).astype(BF16)
        other = swapped(pass_on(other, 1)).astype(F32)
        return pass_on(own, 1).astype(F32) + partial[-1] + other

    residual = (hidden.astype(F32) + ring_sums(partial, first)).astype(BF16)
    normed = rms_scale(residual.astype(F32), norm_gain).astype(BF16)

    def serve(pieces, kinds, digits):
        total = None
        for local in range(local_experts):
            plain = kinds if local_experts == 1 else [F32] * len(kinds)
            served = experts(pieces, plain, digits, own_experts, other_experts, local)
            total = served if local == 0 else [a + b for a, b in zip(total, served)]
        return [part.astype(kind) for part, kind in zip(total, kinds)]

    own, other = normed, swapped(normed)
    pieces = [own]
    for offset in range(1, hops):
        own, other = pass_on(own, -1), pass_on(other, -1)
        pieces = [own, other] + pieces
    pieces = [pass_on(own, -1)] + pieces
    digits = [arrived[offset] for offset in range(hops, -1, -1)]
    nearer = serve(pieces[3:], kinds[3:], digits[2:])
    pieces[1], pieces[2], nearer = lax.optimization_barrier((pieces[1], pieces[2], nearer))
    total = serve(pieces[:3], kinds[:3], digits[:2]) + nearer
    return (residual.astype(F32) + ring_sums(total, pass_on(total[0], 2))).astype(BF16)


def solution(mesh):
    in_specs = (
        P(("groups", "rows"), None),
        P(("groups", "rows"), None, None, None),
        P(("groups", "rows"), None, None, None),
        P(("groups", "rows")),
        P(("groups", "rows"), None),
        P("rows", None),
        P(),
        P("rows", None, None),
        P("rows", None, None),
        P("rows", None, None),
        P(("groups", "rows"), None),
        P(("groups", "rows"), None),
    )
    out_specs = P(("groups", "rows"), None)
    return jax.shard_map(
        on_device, mesh=mesh, in_specs=in_specs, out_specs=out_specs, check_vma=False
    )
```
